256 devices in a mesh: row: 8 (over y, x_lo), col: 32 (over z, x_hi, core).
Axes of the slice: x: 4 (x_hi: 2, x_lo: 2; x = x_hi * 2 + x_lo), y: 4, z: 8, core: 2. Of those that a mesh axis runs over, the one named last changes fastest.
Arguments:
- weight_change: bfloat16 [8192, 28672], P('row', 'col'), may hold values from -6 to 6
- error_buffer: float32 [8192, 28672], P('row', 'col'), may hold values from -6 to 6
- basis: float32 [28672, 64], P('col'), may hold values from -6 to 6
- rollout_weight: bfloat16 [8192, 28672], P('col', 'row'), may hold values from -1.5 to 1.5
Outputs:
- new_error: float32 [8192, 28672], P('row', 'col')
- new_basis: float32 [28672, 64], P('col')
- new_rollout: bfloat16 [8192, 28672], P('col', 'row')
The draws below stay inside these ranges and needn't reach their ends.
All inputs are finite; a program needn't handle non-finite values.
Results may differ from the reference program's by a relative error of at most 0.0057.
Values may be sent and summed in bfloat16 or wider, within the bound.
No kernel may reach another device: no remote copies, remote signals or barrier semaphores. Data moves between devices by JAX's collectives and lax.ppermute only.
A program may use at most 64 MiB of HBM per device.

```python
import jax
import jax.numpy as jnp
from jax import lax

D = 8192
FF = 28672
R = 64


def block_levels(stream_key, dims, split, smallest, largest):
    def one(dim, shards_of):
        heights = jax.random.uniform(jax.random.fold_in(jax.random.fold_in(stream_key, 6), dim), (shards_of,), jnp.float32, smallest / len(split), largest / len(split))
        return jnp.repeat(jnp.exp(heights), dims[dim] // shards_of).reshape((-1,) + (1,) * (len(dims) - dim - 1))

    loudness = one(*split[0])
    for cut in split[1:]:
        loudness = loudness * one(*cut)
    return loudness


def bell_draw(rng, shape, deviation, bound, shards=(), held_as=jnp.bfloat16):
    result = jax.random.normal(rng, shape, jnp.float32) * deviation
    if len(shards) > 0:
        result = block_levels(rng, shape, shards, -0.22, 0.18) * result
    return jnp.clip(result, min=-bound, max=bound).astype(held_as)


def setup_inputs(seed: int = 0) -> dict:
    seeds = jax.random.split(jax.random.key(seed), 5)
    weight_change = bell_draw(seeds[0], (D, FF), 1.0, 6.0, ((0, 8), (1, 32)))
    error_buffer = bell_draw(seeds[1], (D, FF), 0.7, 6.0, ((0, 8), (1, 32)), jnp.float32)
    basis = bell_draw(seeds[2], (FF, R), 1.0, 6.0, ((0, 32),), jnp.float32)
    rollout_weight = bell_draw(seeds[3], (D, FF), 0.1, 1.5, ((0, 32), (1, 8)))
    return dict(weight_change=weight_change, error_buffer=error_buffer, basis=basis, rollout_weight=rollout_weight)


def reference(weight_change, error_buffer, basis, rollout_weight):
    total = weight_change.astype(jnp.float32) + error_buffer
    left = jnp.dot(total.astype(jnp.float32), basis.astype(jnp.float32), precision=lax.Precision.HIGHEST, preferred_element_type=jnp.float32)
    gram = jnp.dot(left.T.astype(jnp.float32), left.astype(jnp.float32), precision=lax.Precision.HIGHEST, preferred_element_type=jnp.float32)
    lower = jnp.linalg.cholesky(gram)
    ortho = lax.linalg.triangular_solve(lower, left, left_side=False, lower=True, transpose_a=True)
    left_round = ortho.astype(jnp.bfloat16)
    new_basis = lax.dot_general(total.astype(jnp.float32), left_round.astype(jnp.float32), (((0,), (0,)), ((), ())), precision=lax.Precision.HIGHEST, preferred_element_type=jnp.float32)
    right_round = new_basis.astype(jnp.bfloat16)
    delta = lax.dot_general(left_round.astype(jnp.float32), right_round.astype(jnp.float32), (((1,), (1,)), ((), ())), preferred_element_type=jnp.float32)
    new_error = total - delta
    new_rollout = (rollout_weight.astype(jnp.float32) + delta).astype(jnp.bfloat16)
    return (new_error, new_basis, new_rollout)
```

```python
import jax
import jax.numpy as jnp
from jax import lax
from jax.sharding import PartitionSpec as P

HIGHEST = lax.Precision.HIGHEST
ROWS, COLS, R = 8, 32, 64
AXES = ("row", "col")


def swap(flip):
    return [
        (r * COLS + c, (c // 4) * COLS + 4 * r + ((c % 4) ^ flip))
        for r in range(ROWS)
        for c in range(COLS)
    ]


def dot(a, b, ca, cb, precision=None):
    return lax.dot_general(
        a, b, (((ca,), (cb,)), ((), ())), precision=precision, preferred_element_type=jnp.float32
    )


def sum_then_share(parts, axis):
    n = parts.shape[0]
    mine = jnp.sum(lax.all_to_all(parts, axis, 0, 0), axis=0)
    return lax.all_to_all(jnp.broadcast_to(mine[None], (n,) + mine.shape), axis, 0, 0)


def local(weight_change, error_buffer, basis, rollout_weight):
    q = lax.axis_index("col") % 4
    total = weight_change.astype(jnp.float32) + error_buffer
    rows, units = total.shape
    part = dot(basis, total, 0, 1, HIGHEST)
    part = part.reshape(8, 8, 4, rows // 4).transpose(0, 2, 1, 3).reshape(COLS, 8, rows // 4)
    left = sum_then_share(part, "col")
    left = left.reshape(8, 4, 8, rows // 4).transpose(0, 2, 1, 3).reshape(R, rows)
    mine = lax.dynamic_slice_in_dim(left, q * (rows // 4), rows // 4, 1)
    my_left = lax.ppermute(mine, AXES, swap(0))
    gram_part = dot(left, left, 1, 1, HIGHEST)
    right_part = dot(left, total, 1, 0, HIGHEST)
    gram_lanes = gram_part.reshape(8, 8, R).transpose(1, 0, 2).reshape(8, 8 * R)
    sent = jnp.concatenate(
        [right_part.reshape(ROWS, 8, units), jnp.broadcast_to(gram_lanes[None], (ROWS, 8, 8 * R))], 2
    )
    got = jnp.sum(lax.all_to_all(sent, "row", 0, 0), axis=0)
    gram = got[:, units:].reshape(8, 8, R).transpose(1, 0, 2).reshape(R, R)
    mine = got[:, :units]
    right = lax.all_to_all(jnp.broadcast_to(mine[None], (ROWS, 8, units)), "row", 0, 0)
    right = right.reshape(R, units)
    lower = jnp.linalg.cholesky(gram)
    inverse = lax.linalg.triangular_solve(
        lower, jnp.eye(R, dtype=jnp.float32), left_side=True, lower=True
    )
    new_basis = dot(inverse, right, 1, 0, HIGHEST)
    right_round = new_basis.astype(jnp.bfloat16)
    blocks = [lax.ppermute(right_round, AXES, swap(k)) for k in range(4)]
    left_round = dot(inverse, left, 1, 0, HIGHEST).astype(jnp.bfloat16)
    delta = dot(left_round, right_round, 0, 0)
    new_error = total - delta
    my_left_round = dot(inverse, my_left, 1, 0, HIGHEST).astype(jnp.bfloat16)
    first = jnp.where((q & 1) == 0, jnp.stack(blocks), jnp.stack([blocks[k ^ 1] for k in range(4)]))
    both = jnp.where((q & 2) == 0, first, jnp.stack([first[k ^ 2] for k in range(4)]))
    my_right = both.transpose(1, 0, 2).reshape(R, 4 * units)
    rollout_delta = dot(my_left_round, my_right, 0, 0)
    new_rollout = (rollout_weight.astype(jnp.float32) + rollout_delta).astype(jnp.bfloat16)
    return (new_error, new_basis.T, new_rollout)


def solution(mesh):
    in_specs = (P("row", "col"), P("row", "col"), P("col", None), P("col", "row"))
    out_specs = (P("row", "col"), P("col", None), P("col", "row"))
    return jax.shard_map(local, mesh=mesh, in_specs=in_specs, out_specs=out_specs, check_vma=False)
```

```python
import jax
import jax.numpy as jnp
from jax import lax
from jax.sharding import PartitionSpec as P

HIGH = lax.Precision.HIGH
HIGHEST = lax.Precision.HIGHEST
ROWS, COLS, R = 8, 32, 64
AXES = ("row", "col")
SWAP = [(r * COLS + c, (c // 4) * COLS + 4 * r + c % 4) for r in range(ROWS) for c in range(COLS)]
SAME_CORE = [[c for c in range(COLS) if c % 2 == core] for core in range(2)]
PAIR = [(c, c ^ 1) for c in range(COLS)]


def dot(a, b, ca, cb, precision=None):
    return lax.dot_general(
        a, b, (((ca,), (cb,)), ((), ())), precision=precision, preferred_element_type=jnp.float32
    )


def exchange(parts, axis, groups=None):
    return lax.all_to_all(parts, axis, 0, 0, axis_index_groups=groups)


def share(mine, n, axis, groups=None):
    return exchange(jnp.broadcast_to(mine[None], (n,) + mine.shape), axis, groups)


def local(weight_change, error_buffer, basis, rollout_weight):
    q = lax.axis_index("col") % 4
    core = q % 2
    total = weight_change.astype(jnp.float32) + error_buffer
    rows, units = total.shape
    part = dot(basis, total, 0, 1, HIGH)
    part = part.reshape(8, 8, 4, rows // 4).transpose(0, 2, 1, 3).reshape(COLS, 8, rows // 4)
    left = share(jnp.sum(exchange(part, "col"), axis=0), COLS, "col")
    left = left.reshape(8, 4, 8, rows // 4).transpose(0, 2, 1, 3).reshape(R, rows)
    mine = lax.dynamic_slice_in_dim(left, q * (rows // 4), rows // 4, 1)
    my_left = lax.ppermute(mine, AXES, SWAP)
    gram_part = dot(left, left, 1, 1, HIGHEST)
    right_part = dot(left, total, 1, 0, HIGH)
    blocks = jnp.pad(right_part, ((0, 0), (0, 128 * ROWS - units))).reshape(R, ROWS, 128).transpose(1, 0, 2)
    gram_part = jnp.concatenate([gram_part[: R // 2], gram_part[R // 2 :]], 1)
    sent = jnp.concatenate([blocks, jnp.broadcast_to(gram_part[None], (ROWS, R // 2, 128))], 1)
    got = jnp.sum(exchange(sent, "row"), axis=0)
    gram = jnp.concatenate([got[R:, :R], got[R:, R:]], 0)
    my_block = got[:R]
    far_block = lax.ppermute(my_block, AXES, SWAP)
    lower = jnp.linalg.cholesky(gram)
    inverse = lax.linalg.triangular_solve(
        lower, jnp.eye(R, dtype=jnp.float32), left_side=True, lower=True
    )
    new_blocks = share(dot(inverse, my_block, 1, 0, HIGHEST), ROWS, "row")
    far_round = dot(inverse, far_block, 1, 0, HIGHEST).astype(jnp.bfloat16)
    near = share(far_round, COLS // 2, "col", SAME_CORE)
    other = lax.ppermute(near, "col", PAIR)
    new_basis = new_blocks.transpose(1, 0, 2).reshape(R, 128 * ROWS)[:, :units]
    left_round = dot(inverse, left, 1, 0, HIGHEST).astype(jnp.bfloat16)
    new_error = total - dot(left_round, new_basis.astype(jnp.bfloat16), 0, 0)
    my_left_round = dot(inverse, my_left, 1, 0, HIGHEST).astype(jnp.bfloat16)
    right = jnp.where(core == 0, jnp.stack([near, other]), jnp.stack([other, near]))
    right = right.reshape(2, 8, 2, R, 128)[:, : units // 128]
    right = right.transpose(3, 2, 0, 1, 4).reshape(R, 4 * units)
    rollout_delta = dot(my_left_round, right, 0, 0)
    new_rollout = (rollout_weight.astype(jnp.float32) + rollout_delta).astype(jnp.bfloat16)
    return (new_error, new_basis.T, new_rollout)


def solution(mesh):
    in_specs = (P("row", "col"), P("row", "col"), P("col", None), P("col", "row"))
    out_specs = (P("row", "col"), P("col", None), P("col", "row"))
    return jax.shard_map(local, mesh=mesh, in_specs=in_specs, out_specs=out_specs, check_vma=False)
```

```python
import jax
import jax.numpy as jnp
from jax import lax
from jax.experimental import pallas as pl
from jax.experimental.pallas import tpu as pltpu
from jax.sharding import PartitionSpec as P

HIGH = lax.Precision.HIGH
HIGHEST = lax.Precision.HIGHEST
ROWS, COLS, R, LANES, BLOCKS = 8, 32, 64, 128, 8
AXES = ("row", "col")
SWAP = [(r * COLS + c, (c // 4) * COLS + 4 * r + c % 4) for r in range(ROWS) for c in range(COLS)]
SAME_CORE = [[c for c in range(COLS) if c % 2 == core] for core in range(2)]
PAIR = [(c, c ^ 1) for c in range(COLS)]


def dot(a, b, ca, cb, precision=None):
    return lax.dot_general(
        a, b, (((ca,), (cb,)), ((), ())), precision=precision, preferred_element_type=jnp.float32
    )


def exchange(parts, axis, groups=None):
    return lax.all_to_all(parts, axis, 0, 0, axis_index_groups=groups)


def share(mine, n, axis, groups=None):
    return exchange(jnp.broadcast_to(mine[None], (n,) + mine.shape), axis, groups)


def inverse_factor(gram):
    n = R // 8
    lane = lax.broadcasted_iota(jnp.int32, (8, R), 1)
    sub = lax.broadcasted_iota(jnp.int32, (8, R), 0)
    wide = [
        jnp.concatenate([gram[8 * i : 8 * i + 8], (lane == sub + 8 * i).astype(jnp.float32)], 1)
        for i in range(n)
    ]
    row = lax.broadcasted_iota(jnp.int32, (8, LANES), 0)
    out = []

    def pick(x, k):
        return jnp.broadcast_to(x[k : k + 1], (8, LANES))

    for p in range(n):
        column = [
            [jnp.broadcast_to(wide[i][:, 8 * p + k : 8 * p + k + 1], (8, LANES)) for i in range(p, n)]
            for k in range(8)
        ]
        scale = jnp.zeros((8, LANES), jnp.float32)
        for k in range(8):
            pivot = pick(column[k][0], k)
            times = 1.0 / pivot
            scale = jnp.where(row == k, lax.rsqrt(pivot), scale)
            by = [c * times for c in column[k]]
            by[0] = jnp.where(row > k, by[0], 0.0)
            for l in range(k + 1, 8):
                value = pick(column[l][0], k)
                column[l] = [c - b * value for c, b in zip(column[l], by)]
            value = pick(wide[p], k)
            for i in range(p, n):
                wide[i] = wide[i] - by[i - p] * value
        out.append(wide[p][:, R:] * scale[:, R:])
    return jnp.concatenate(out, 0)


def factor_kernel(got_ref, inverse_ref, blocks_ref):
    packed = got_ref[R:]
    gram = jnp.concatenate([packed[:, :R], packed[:, R:]], 0)
    inverse = inverse_factor(gram)
    inverse_ref[...] = inverse
    block = dot(inverse, got_ref[:R], 1, 0, HIGHEST)
    for b in range(BLOCKS):
        blocks_ref[b] = block


def factor(got):
    return pl.pallas_call(
        factor_kernel,
        out_shape=[
            jax.ShapeDtypeStruct((R, R), jnp.float32),
            jax.ShapeDtypeStruct((BLOCKS, R, LANES), jnp.float32),
        ],
        cost_estimate=pl.CostEstimate(flops=10**7, bytes_accessed=20 * 10**6, transcendentals=0),
        name="factor",
    )(got)


def far_kernel(inverse_ref, block_ref, out_ref):
    block = dot(inverse_ref[...], block_ref[...], 1, 0, HIGHEST).astype(jnp.bfloat16)
    for b in range(out_ref.shape[0]):
        out_ref[b] = block


def far_blocks(inverse, block):
    return pl.pallas_call(
        far_kernel,
        out_shape=jax.ShapeDtypeStruct((COLS // 2, R, LANES), jnp.bfloat16),
        name="far_blocks",
    )(inverse, block)


def rollout_kernel(core_ref, inverse_ref, left_ref, near_ref, other_ref, weight_ref, out_ref, round_ref):
    i = pl.program_id(0)

    @pl.when(i == 0)
    def _():
        ortho = dot(left_ref[...], inverse_ref[...], 0, 1, HIGHEST)
        round_ref[...] = ortho.astype(jnp.bfloat16)

    def write(right_ref):
        half = i // 2
        for b in range(out_ref.shape[1] // LANES):
            lanes = pl.ds(b * LANES, LANES)
            delta = dot(round_ref[...], right_ref[b, half], 1, 0)
            out_ref[:, lanes] = (weight_ref[:, lanes].astype(jnp.float32) + delta).astype(jnp.bfloat16)

    @pl.when(i % 2 == core_ref[0])
    def _():
        write(near_ref)

    @pl.when(i % 2 != core_ref[0])
    def _():
        write(other_ref)


def rollout(core, inverse, left, near, other, weight):
    rows, units = weight.shape
    right = pl.BlockSpec((BLOCKS, 2, R, LANES), lambda i, core: (0, 0, 0, 0))
    block = pl.BlockSpec((rows, units // 4), lambda i, core: (0, i))
    return pl.pallas_call(
        rollout_kernel,
        grid_spec=pltpu.PrefetchScalarGridSpec(
            num_scalar_prefetch=1,
            grid=(4,),
            in_specs=[
                pl.BlockSpec((R, R), lambda i, core: (0, 0)),
                pl.BlockSpec((R, rows), lambda i, core: (0, 0)),
                right,
                right,
                block,
            ],
            out_specs=block,
            scratch_shapes=[pltpu.VMEM((rows, R), jnp.bfloat16)],
        ),
        out_shape=jax.ShapeDtypeStruct((rows, units), jnp.bfloat16),
        name="rollout",
    )(core, inverse, left, near, other, weight)


def local(weight_change, error_buffer, basis, rollout_weight):
    q = lax.axis_index("col") % 4
    core = q % 2
    total = weight_change.astype(jnp.float32) + error_buffer
    rows, units = total.shape
    part = dot(basis, total, 0, 1, HIGH)
    part = part.reshape(8, 8, 4, rows // 4).transpose(0, 2, 1, 3).reshape(COLS, 8, rows // 4)
    left = share(jnp.sum(exchange(part, "col"), axis=0), COLS, "col")
    left = left.reshape(8, 4, 8, rows // 4).transpose(0, 2, 1, 3).reshape(R, rows)
    mine = lax.dynamic_slice_in_dim(left, q * (rows // 4), rows // 4, 1)
    my_left = lax.ppermute(mine, AXES, SWAP)
    gram_part = dot(left, left, 1, 1, HIGHEST)
    right_part = dot(left, total, 1, 0, HIGH)
    blocks = jnp.pad(right_part, ((0, 0), (0, LANES * BLOCKS - units)))
    blocks = blocks.reshape(R, BLOCKS, LANES).transpose(1, 0, 2)
    gram_part = jnp.concatenate([gram_part[: R // 2], gram_part[R // 2 :]], 1)
    sent = jnp.concatenate([blocks, jnp.broadcast_to(gram_part[None], (BLOCKS, R // 2, LANES))], 1)
    got = jnp.sum(exchange(sent, "row"), axis=0)
    got, my_left = lax.optimization_barrier((got, my_left))
    far_block = lax.ppermute(got[:R], AXES, SWAP)
    inverse, new_blocks = factor(got)
    far = far_blocks(inverse, far_block)
    new_blocks, far = lax.optimization_barrier((new_blocks, far))
    near = exchange(far, "col", SAME_CORE)
    other = lax.ppermute(near, "col", PAIR)
    new_basis = exchange(new_blocks, "row").transpose(1, 0, 2).reshape(R, LANES * BLOCKS)[:, :units]
    left_round = dot(inverse, left, 1, 0, HIGHEST).astype(jnp.bfloat16)
    new_error = total - dot(left_round, new_basis.astype(jnp.bfloat16), 0, 0)
    halves = (BLOCKS, 2, R, LANES)
    new_rollout = rollout(
        core.astype(jnp.int32).reshape(1), inverse, my_left, near.reshape(halves), other.reshape(halves), rollout_weight
    )
    return (new_error, new_basis.T, new_rollout)


def solution(mesh):
    in_specs = (P("row", "col"), P("row", "col"), P("col", None), P("col", "row"))
    out_specs = (P("row", "col"), P("col", None), P("col", "row"))
    return jax.shard_map(local, mesh=mesh, in_specs=in_specs, out_specs=out_specs, check_vma=False)
```

```python
import jax
import jax.numpy as jnp
from jax import lax
from jax.experimental import pallas as pl
from jax.experimental.pallas import tpu as pltpu
from jax.sharding import PartitionSpec as P

HIGH = lax.Precision.HIGH
HIGHEST = lax.Precision.HIGHEST
ROWS, COLS, R, LANES, BLOCKS = 8, 32, 64, 128, 8
AXES = ("row", "col")
SWAP = [(r * COLS + c, (c // 4) * COLS + 4 * r + c % 4) for r in range(ROWS) for c in range(COLS)]
SAME_CORE = [[c for c in range(COLS) if c % 2 == core] for core in range(2)]
PAIR = [(c, c ^ 1) for c in range(COLS)]


def dot(a, b, ca, cb, precision=None):
    return lax.dot_general(
        a, b, (((ca,), (cb,)), ((), ())), precision=precision, preferred_element_type=jnp.float32
    )


def split(x):
    hi = x.astype(jnp.bfloat16)
    return hi, (x - hi.astype(jnp.float32)).astype(jnp.bfloat16)


def exchange(parts, axis, groups=None):
    return lax.all_to_all(parts, axis, 0, 0, axis_index_groups=groups)


def share(mine, n, axis, groups=None):
    return exchange(jnp.broadcast_to(mine[None], (n,) + mine.shape), axis, groups)


ANY = pl.BlockSpec(memory_space=pl.ANY)
VMEM = pl.BlockSpec(memory_space=pltpu.VMEM)
SMEM = pl.BlockSpec(memory_space=pltpu.SMEM)


def grant(mib):
    return pltpu.CompilerParams(vmem_limit_bytes=mib * 2**20)


def left_kernel(change_ref, error_ref, basis_ref, out_ref, change_buf, error_buf, basis_buf, sem, basis_sem):
    rows, width = change_ref.shape[0], out_ref.shape[3]
    block = rows // 2
    basis_copy = pltpu.make_async_copy(basis_ref, basis_buf, basis_sem)
    basis_copy.start()
    copies = []
    for i in range(2):
        part = pl.ds(i * block, block)
        pair = [
            pltpu.make_async_copy(change_ref.at[part], change_buf.at[part], sem.at[0, i]),
            pltpu.make_async_copy(error_ref.at[part], error_buf.at[part], sem.at[1, i]),
        ]
        for copy in pair:
            copy.start()
        copies.append(pair)
    basis_copy.wait()
    basis_hi, basis_lo = split(basis_buf[...])
    basis_both = jnp.concatenate([basis_hi, basis_lo], 0)
    for i in range(2):
        for copy in copies[i]:
            copy.wait()
        part = pl.ds(i * block, block)
        hi, lo = split(change_buf[part].astype(jnp.float32) + error_buf[part])
        both = dot(basis_both, hi, 1, 1)
        left = both[:R] + both[R:] + dot(basis_hi, lo, 1, 1)
        for j in range(block // width):
            out_ref[:, i * (block // width) + j] = left[:, j * width : (j + 1) * width].reshape(8, 8, width)


def left_part(change, error, basis):
    rows, units = change.shape
    return pl.pallas_call(
        left_kernel,
        in_specs=[ANY, ANY, ANY],
        out_specs=VMEM,
        out_shape=jax.ShapeDtypeStruct((8, 4, 8, rows // 4), jnp.float32),
        scratch_shapes=[
            pltpu.VMEM((rows, units), jnp.bfloat16),
            pltpu.VMEM((rows, units), jnp.float32),
            pltpu.VMEM((R, units), jnp.float32),
            pltpu.SemaphoreType.DMA((2, 2)),
            pltpu.SemaphoreType.DMA,
        ],
        compiler_params=grant(62),
        cost_estimate=pl.CostEstimate(flops=6 * rows * units * R, bytes_accessed=6 * rows * units, transcendentals=0),
        name="left_part",
    )(change, error, basis)


def right_kernel(hi_ref, lo_ref, left_ref, out_ref):
    left = jnp.concatenate([left_ref[:, i].reshape(R, -1) for i in range(4)], 1)
    left_hi, left_lo = split(left)
    both = dot(jnp.concatenate([left_hi, left_lo], 0), hi_ref[...], 1, 0)
    right = both[:R] + both[R:] + dot(left_hi, lo_ref[...], 1, 0)
    used = right.shape[1] // LANES
    for b in range(used):
        out_ref[b, :R] = right[:, b * LANES : (b + 1) * LANES]
    for b in range(used, BLOCKS):
        out_ref[b, :R] = jnp.zeros((R, LANES), jnp.float32)
    gram = dot(left, left, 1, 1, HIGHEST)
    for b in range(BLOCKS):
        out_ref[b, R:, :R] = gram[: R // 2]
        out_ref[b, R:, R:] = gram[R // 2 :]


def right_part(hi, lo, left):
    rows, units = hi.shape
    return pl.pallas_call(
        right_kernel,
        in_specs=[VMEM, VMEM, VMEM],
        out_specs=VMEM,
        out_shape=jax.ShapeDtypeStruct((BLOCKS, R + R // 2, LANES), jnp.float32),
        compiler_params=grant(12),
        cost_estimate=pl.CostEstimate(flops=6 * rows * units * R, bytes_accessed=4 * rows * units, transcendentals=0),
        name="right_part",
    )(hi, lo, left)


def inverse_factor(gram):
    n = R // 8
    lane = lax.broadcasted_iota(jnp.int32, (8, R), 1)
    sub = lax.broadcasted_iota(jnp.int32, (8, R), 0)
    wide = [
        jnp.concatenate([gram[8 * i : 8 * i + 8], (lane == sub + 8 * i).astype(jnp.float32)], 1)
        for i in range(n)
    ]
    row = lax.broadcasted_iota(jnp.int32, (8, LANES), 0)
    out = []

    def pick(x, k):
        return jnp.broadcast_to(x[k : k + 1], (8, LANES))

    for p in range(n):
        column = [
            [jnp.broadcast_to(wide[i][:, 8 * p + k : 8 * p + k + 1], (8, LANES)) for i in range(p, n)]
            for k in range(8)
        ]
        scale = jnp.zeros((8, LANES), jnp.float32)
        for k in range(8):
            pivot = pick(column[k][0], k)
            times = 1.0 / pivot
            scale = jnp.where(row == k, lax.rsqrt(pivot), scale)
            by = [c * times for c in column[k]]
            by[0] = jnp.where(row > k, by[0], 0.0)
            for l in range(k + 1, 8):
                value = pick(column[l][0], k)
                column[l] = [c - b * value for c, b in zip(column[l], by)]
            value = pick(wide[p], k)
            for i in range(p, n):
                wide[i] = wide[i] - by[i - p] * value
        out.append(wide[p][:, R:] * scale[:, R:])
    return jnp.concatenate(out, 0)


def settle_kernel(q_ref, parts_ref, left_ref, blocks_ref, sent_ref, gram_ref):
    got = parts_ref[0]
    for b in range(1, BLOCKS):
        got = got + parts_ref[b]
    sent_ref[:, :LANES] = got[:R]
    for b in range(BLOCKS):
        blocks_ref[b] = got[:R]
    gram_ref[...] = got[R:]
    sent_ref[:, LANES:] = left_ref[:, q_ref[0]].reshape(R, left_ref.shape[3])


def settle(q, parts, left):
    return pl.pallas_call(
        settle_kernel,
        in_specs=[SMEM, VMEM, VMEM],
        out_specs=[VMEM, VMEM, VMEM],
        out_shape=[
            jax.ShapeDtypeStruct((BLOCKS, R, LANES), jnp.float32),
            jax.ShapeDtypeStruct((R, LANES + left.shape[3]), jnp.float32),
            jax.ShapeDtypeStruct((R // 2, LANES), jnp.float32),
        ],
        compiler_params=grant(6),
        name="settle",
    )(q, parts, left)


def factor_kernel(gram_ref, inverse_ref, copies_ref):
    packed = gram_ref[...]
    inverse = inverse_factor(jnp.concatenate([packed[:, :R], packed[:, R:]], 0))
    inverse_ref[...] = inverse
    for b in range(copies_ref.shape[0] // R):
        copies_ref[b * R : (b + 1) * R] = inverse


def factor(gram):
    return pl.pallas_call(
        factor_kernel,
        in_specs=[VMEM],
        out_specs=[VMEM, VMEM],
        out_shape=[
            jax.ShapeDtypeStruct((R, R), jnp.float32),
            jax.ShapeDtypeStruct((COLS // 2 * R, R), jnp.float32),
        ],
        compiler_params=grant(6),
        cost_estimate=pl.CostEstimate(flops=10**7, bytes_accessed=20 * 10**6, transcendentals=0),
        name="factor",
    )(gram)


def rollout_kernel(core_ref, left_ref, near_ref, other_ref, weight_ref, out_ref, buf, sem):
    even = core_ref[0] == 0
    width = buf.shape[2]
    copies = []
    for q in range(4):
        first, second = (near_ref, other_ref) if q % 2 == 0 else (other_ref, near_ref)
        blocks = [jnp.where(even, first[b, q // 2], second[b, q // 2]) for b in range(width // LANES)]
        delta = dot(left_ref[...], jnp.concatenate(blocks, 1), 1, 0)
        buf[q] = (weight_ref[q].astype(jnp.float32) + delta).astype(jnp.bfloat16)
        copy = pltpu.make_async_copy(buf.at[q], out_ref.at[:, pl.ds(q * width, width)], sem.at[q])
        copy.start()
        copies.append(copy)
    for copy in copies:
        copy.wait()


def rollout(core, left, near, other, weight):
    quarters, rows, width = weight.shape
    return pl.pallas_call(
        rollout_kernel,
        in_specs=[SMEM, VMEM, VMEM, VMEM, VMEM],
        out_specs=ANY,
        out_shape=jax.ShapeDtypeStruct((rows, quarters * width), jnp.bfloat16),
        scratch_shapes=[
            pltpu.VMEM((quarters, rows, width), jnp.bfloat16),
            pltpu.SemaphoreType.DMA((4,)),
        ],
        compiler_params=grant(12),
        name="rollout",
    )(core, left, near, other, weight)


def local(weight_change, error_buffer, basis, rollout_weight):
    q = lax.axis_index("col") % 4
    core = q % 2
    rows, units = weight_change.shape
    part = left_part(weight_change, error_buffer, basis.T)
    part, change, error = lax.optimization_barrier((part, weight_change, error_buffer))
    hi, lo = split(change.astype(jnp.float32) + error)
    mine = jnp.sum(exchange(part.reshape(COLS, 8, rows // 4), "col"), axis=0)
    mine, hi, lo, weight = lax.optimization_barrier((mine, hi, lo, rollout_weight))
    weight = weight.reshape(weight.shape[0], 4, units).transpose(1, 0, 2)
    left = share(mine, COLS, "col").reshape(8, 4, 8, rows // 4)
    left, weight = lax.optimization_barrier((left, weight))
    parts = exchange(right_part(hi, lo, left), "row")
    blocks, sent, gram = settle(q.astype(jnp.int32).reshape(1), parts, left)
    far = lax.ppermute(sent, AXES, SWAP)
    blocks = exchange(blocks, "row")
    inverse, copies = factor(gram)
    far, blocks, copies = lax.optimization_barrier((far, blocks, copies))
    far_round = dot(copies, far[:, :LANES], 1, 0, HIGH).astype(jnp.bfloat16).reshape(COLS // 2, R, LANES)
    far_round, inverse = lax.optimization_barrier((far_round, inverse))
    near = exchange(far_round, "col", SAME_CORE)
    right = blocks.transpose(1, 0, 2).reshape(R, LANES * BLOCKS)[:, :units]
    new_basis = dot(inverse, right, 1, 0, HIGH)
    left_rows = left.transpose(0, 2, 1, 3).reshape(R, rows)
    left_round = dot(inverse, left_rows, 1, 0, HIGH).astype(jnp.bfloat16)
    total = weight_change.astype(jnp.float32) + error_buffer
    new_error = total - dot(left_round, new_basis.astype(jnp.bfloat16), 0, 0)
    far_left = dot(far[:, LANES:], inverse, 0, 1, HIGH).astype(jnp.bfloat16)
    near, new_error, far_left = lax.optimization_barrier((near, new_error, far_left))
    other = lax.ppermute(near, "col", PAIR)
    halves = (BLOCKS, 2, R, LANES)
    new_rollout = rollout(
        core.astype(jnp.int32).reshape(1), far_left, near.reshape(halves), other.reshape(halves), weight
    )
    return (new_error, new_basis.T, new_rollout)


def solution(mesh):
    in_specs = (P("row", "col"), P("row", "col"), P("col", None), P("col", "row"))
    out_specs = (P("row", "col"), P("col", None), P("col", "row"))
    return jax.shard_map(local, mesh=mesh, in_specs=in_specs, out_specs=out_specs, check_vma=False)
```

```python
import jax
import jax.numpy as jnp
from jax import lax
from jax.experimental import pallas as pl
from jax.experimental.pallas import tpu as pltpu
from jax.sharding import PartitionSpec as P

HIGH = lax.Precision.HIGH
HIGHEST = lax.Precision.HIGHEST
ROWS, COLS, R, LANES, BLOCKS = 8, 32, 64, 128, 8
AXES = ("row", "col")


def row_hops(a, b):
    y = abs(a // 2 - b // 2)
    return min(y, 4 - y) + abs(a % 2 - b % 2)


def partners(row):
    rows = sorted(range(ROWS), key=lambda r: (row_hops(r, row), r))
    places = sorted(range(8), key=lambda k: (-min(k, 8 - k), k))
    return {r: (row + k) % 8 for r, k in zip(rows, places)}


SLOTS = [[partners(z)[r] for r in range(ROWS)] for z in range(8)]
SPREAD = [
    (r * COLS + 4 * z + q, z * COLS + 4 * SLOTS[z][r] + q)
    for r in range(ROWS)
    for z in range(8)
    for q in range(4)
]
FANOUT = [
    (r * COLS + 4 * z + q, t * COLS + 4 * r + q)
    for r in range(ROWS)
    for t, z in partners(r).items()
    for q in range(4)
]
SAME_CORE = [[c for c in range(COLS) if c % 2 == core] for core in range(2)]
PAIR = [(c, c ^ 1) for c in range(COLS)]


def dot(a, b, ca, cb, precision=None):
    return lax.dot_general(
        a, b, (((ca,), (cb,)), ((), ())), precision=precision, preferred_element_type=jnp.float32
    )


def split(x):
    hi = x.astype(jnp.bfloat16)
    return hi, (x - hi.astype(jnp.float32)).astype(jnp.bfloat16)


def exchange(parts, axis, groups=None):
    return lax.all_to_all(parts, axis, 0, 0, axis_index_groups=groups)


ANY = pl.BlockSpec(memory_space=pl.ANY)
VMEM = pl.BlockSpec(memory_space=pltpu.VMEM)
SMEM = pl.BlockSpec(memory_space=pltpu.SMEM)


def grant(mib):
    return pltpu.CompilerParams(vmem_limit_bytes=mib * 2**20)


def left_kernel(change_ref, error_ref, basis_ref, out_ref, change_buf, error_buf, basis_buf, sem, basis_sem):
    rows, width = change_ref.shape[0], out_ref.shape[3]
    block = rows // 2
    basis_copy = pltpu.make_async_copy(basis_ref, basis_buf, basis_sem)
    basis_copy.start()
    copies = []
    for i in range(2):
        part = pl.ds(i * block, block)
        pair = [
            pltpu.make_async_copy(change_ref.at[part], change_buf.at[part], sem.at[0, i]),
            pltpu.make_async_copy(error_ref.at[part], error_buf.at[part], sem.at[1, i]),
        ]
        for copy in pair:
            copy.start()
        copies.append(pair)
    basis_copy.wait()
    basis_hi, basis_lo = split(basis_buf[...])
    basis_both = jnp.concatenate([basis_hi, basis_lo], 0)
    for i in range(2):
        for copy in copies[i]:
            copy.wait()
        part = pl.ds(i * block, block)
        hi, lo = split(change_buf[part].astype(jnp.float32) + error_buf[part])
        both = dot(basis_both, hi, 1, 1)
        left = both[:R] + both[R:] + dot(basis_hi, lo, 1, 1)
        for j in range(block // width):
            out_ref[:, i * (block // width) + j] = left[:, j * width : (j + 1) * width].reshape(8, 8, width)


def left_part(change, error, basis):
    rows, units = change.shape
    return pl.pallas_call(
        left_kernel,
        in_specs=[ANY, ANY, ANY],
        out_specs=VMEM,
        out_shape=jax.ShapeDtypeStruct((8, 4, 8, rows // 4), jnp.float32),
        scratch_shapes=[
            pltpu.VMEM((rows, units), jnp.bfloat16),
            pltpu.VMEM((rows, units), jnp.float32),
            pltpu.VMEM((R, units), jnp.float32),
            pltpu.SemaphoreType.DMA((2, 2)),
            pltpu.SemaphoreType.DMA,
        ],
        compiler_params=grant(62),
        cost_estimate=pl.CostEstimate(flops=6 * rows * units * R, bytes_accessed=6 * rows * units, transcendentals=0),
        name="left_part",
    )(change, error, basis)


def sum_share_kernel(parts_ref, out_ref):
    total = parts_ref[0]
    for i in range(1, parts_ref.shape[0]):
        total = total + parts_ref[i]
    for i in range(out_ref.shape[0]):
        out_ref[i] = total


def sum_share(parts):
    return pl.pallas_call(
        sum_share_kernel,
        in_specs=[VMEM],
        out_specs=VMEM,
        out_shape=jax.ShapeDtypeStruct(parts.shape, parts.dtype),
        compiler_params=grant(6),
        name="sum_share",
    )(parts)


def right_kernel(total_ref, left_ref, out_ref):
    left = jnp.concatenate([left_ref[:, i].reshape(R, -1) for i in range(4)], 1)
    both = dot(jnp.concatenate(split(left), 0), total_ref[...], 1, 0)
    right = both[:R] + both[R:]
    used = right.shape[1] // LANES
    for b in range(used):
        out_ref[b, :R] = right[:, b * LANES : (b + 1) * LANES]
    for b in range(used, BLOCKS):
        out_ref[b, :R] = jnp.zeros((R, LANES), jnp.float32)
    gram = dot(left, left, 1, 1, HIGHEST)
    for b in range(BLOCKS):
        out_ref[b, R:, :R] = gram[: R // 2]
        out_ref[b, R:, R:] = gram[R // 2 :]


def right_part(total, left):
    rows, units = total.shape
    return pl.pallas_call(
        right_kernel,
        in_specs=[VMEM, VMEM],
        out_specs=VMEM,
        out_shape=jax.ShapeDtypeStruct((BLOCKS, R + R // 2, LANES), jnp.float32),
        compiler_params=grant(12),
        cost_estimate=pl.CostEstimate(flops=4 * rows * units * R, bytes_accessed=2 * rows * units, transcendentals=0),
        name="right_part",
    )(total, left)


def inverse_factor(gram):
    n = R // 8
    lane = lax.broadcasted_iota(jnp.int32, (8, R), 1)
    sub = lax.broadcasted_iota(jnp.int32, (8, R), 0)
    wide = [
        jnp.concatenate([gram[8 * i : 8 * i + 8], (lane == sub + 8 * i).astype(jnp.float32)], 1)
        for i in range(n)
    ]
    row = lax.broadcasted_iota(jnp.int32, (8, LANES), 0)
    out = []

    def pick(x, k):
        return jnp.broadcast_to(x[k : k + 1], (8, LANES))

    for p in range(n):
        column = [
            [jnp.broadcast_to(wide[i][:, 8 * p + k : 8 * p + k + 1], (8, LANES)) for i in range(p, n)]
            for k in range(8)
        ]
        scale = jnp.zeros((8, LANES), jnp.float32)
        for k in range(8):
            pivot = pick(column[k][0], k)
            times = 1.0 / pivot
            scale = jnp.where(row == k, lax.rsqrt(pivot), scale)
            by = [c * times for c in column[k]]
            by[0] = jnp.where(row > k, by[0], 0.0)
            for l in range(k + 1, 8):
                value = pick(column[l][0], k)
                column[l] = [c - b * value for c, b in zip(column[l], by)]
            value = pick(wide[p], k)
            for i in range(p, n):
                wide[i] = wide[i] - by[i - p] * value
        out.append(wide[p][:, R:] * scale[:, R:])
    return jnp.concatenate(out, 0)


def settle_kernel(parts_ref, block_ref, gram_ref):
    got = parts_ref[0]
    for b in range(1, BLOCKS):
        got = got + parts_ref[b]
    block_ref[...] = got[:R]
    gram_ref[...] = got[R:]


def settle(parts):
    return pl.pallas_call(
        settle_kernel,
        in_specs=[VMEM],
        out_specs=[VMEM, VMEM],
        out_shape=[
            jax.ShapeDtypeStruct((R, LANES), jnp.float32),
            jax.ShapeDtypeStruct((R // 2, LANES), jnp.float32),
        ],
        compiler_params=grant(6),
        name="settle",
    )(parts)


def factor_kernel(gram_ref, inverse_ref, copies_ref):
    packed = gram_ref[...]
    inverse = inverse_factor(jnp.concatenate([packed[:, :R], packed[:, R:]], 0))
    inverse_ref[...] = inverse
    for b in range(copies_ref.shape[0] // R):
        copies_ref[b * R : (b + 1) * R] = inverse


def factor(gram):
    return pl.pallas_call(
        factor_kernel,
        in_specs=[VMEM],
        out_specs=[VMEM, VMEM],
        out_shape=[
            jax.ShapeDtypeStruct((R, R), jnp.float32),
            jax.ShapeDtypeStruct((COLS // 2 * R, R), jnp.float32),
        ],
        compiler_params=grant(6),
        cost_estimate=pl.CostEstimate(flops=10**7, bytes_accessed=20 * 10**6, transcendentals=0),
        name="factor",
    )(gram)


def basis_kernel(row_ref, inverse_ref, mine_ref, other_ref, basis_ref, round_ref):
    y, odd = row_ref[0] // 2, row_ref[0] % 2
    blocks = []
    for b in range(basis_ref.shape[1] // LANES):
        value = jnp.zeros((R, LANES), jnp.float32)
        for k in range(4):
            lanes = slice(k * LANES, (k + 1) * LANES)
            picked = jnp.where(odd == b % 2, mine_ref[:, lanes], other_ref[:, lanes])
            value = jnp.where((y + 4 - k) % 4 == b // 2, picked, value)
        blocks.append(value)
    basis = dot(inverse_ref[...], jnp.concatenate(blocks, 1), 1, 0, HIGHEST)
    basis_ref[...] = basis
    round_ref[...] = basis.astype(jnp.bfloat16)


def basis_part(row, inverse, mine, other, units):
    return pl.pallas_call(
        basis_kernel,
        in_specs=[SMEM] + [VMEM] * 3,
        out_specs=[VMEM, VMEM],
        out_shape=[
            jax.ShapeDtypeStruct((R, units), jnp.float32),
            jax.ShapeDtypeStruct((R, units), jnp.bfloat16),
        ],
        compiler_params=grant(6),
        name="basis_part",
    )(row, inverse, mine, other)


def rollout_kernel(core_ref, slots_ref, left_ref, near_ref, other_ref, weight_ref, out_ref, buf, sem):
    even = core_ref[0] == 0
    width = buf.shape[2]
    copies = []
    for q in range(4):
        first, second = (near_ref, other_ref) if q % 2 == 0 else (other_ref, near_ref)
        blocks = []
        for b in range(width // LANES):
            slot = slots_ref[b]
            blocks.append(jnp.where(even, first[slot, q // 2], second[slot, q // 2]))
        delta = dot(left_ref[...], jnp.concatenate(blocks, 1), 1, 0)
        buf[q] = (weight_ref[q].astype(jnp.float32) + delta).astype(jnp.bfloat16)
        copy = pltpu.make_async_copy(buf.at[q], out_ref.at[:, pl.ds(q * width, width)], sem.at[q])
        copy.start()
        copies.append(copy)
    for copy in copies:
        copy.wait()


def rollout(core, slots, left, near, other, weight):
    quarters, rows, width = weight.shape
    return pl.pallas_call(
        rollout_kernel,
        in_specs=[SMEM, SMEM, VMEM, VMEM, VMEM, VMEM],
        out_specs=ANY,
        out_shape=jax.ShapeDtypeStruct((rows, quarters * width), jnp.bfloat16),
        scratch_shapes=[
            pltpu.VMEM((quarters, rows, width), jnp.bfloat16),
            pltpu.SemaphoreType.DMA((4,)),
        ],
        compiler_params=grant(12),
        name="rollout",
    )(core, slots, left, near, other, weight)


def local(weight_change, error_buffer, basis, rollout_weight):
    row = lax.axis_index("row")
    q = lax.axis_index("col") % 4
    core = q % 2
    rows, units = weight_change.shape
    part = left_part(weight_change, error_buffer, basis.T)
    part, change, error = lax.optimization_barrier((part, weight_change, error_buffer))
    total = (change.astype(jnp.float32) + error).astype(jnp.bfloat16)
    parts = exchange(part.reshape(COLS, 8, rows // 4), "col")
    parts, total = lax.optimization_barrier((parts, total))
    left = exchange(sum_share(parts), "col").reshape(8, 4, 8, rows // 4)
    sums, weight = lax.optimization_barrier((right_part(total, left), rollout_weight))
    weight = jnp.stack([weight[:, i * units : (i + 1) * units] for i in range(4)])
    mine = lax.dynamic_index_in_dim(left, q, 1, keepdims=False).reshape(R, rows // 4)
    far_left = lax.ppermute(mine, AXES, FANOUT)
    parts, weight, far_left = lax.optimization_barrier((exchange(sums, "row"), weight, far_left))
    block, gram = settle(parts)
    far = lax.ppermute(block, AXES, SPREAD)
    blocks = [lax.ppermute(block, "row", [(r, (r + 2 * k) % ROWS) for r in range(ROWS)]) for k in (1, 2, 3)]
    inverse, copies = factor(gram)
    far_round = dot(copies, far, 1, 0, HIGH).astype(jnp.bfloat16).reshape(COLS // 2, R, LANES)
    blocks = jnp.concatenate([block] + blocks, 1)
    far_round, inverse, blocks = lax.optimization_barrier((far_round, inverse, blocks))
    near = exchange(far_round, "col", SAME_CORE)
    other_blocks = lax.ppermute(blocks, "row", [(r, r ^ 1) for r in range(ROWS)])
    left_rows = left.transpose(0, 2, 1, 3).reshape(R, rows)
    left_round = dot(inverse, left_rows, 1, 0, HIGH).astype(jnp.bfloat16)
    far_left = dot(far_left, inverse, 0, 1, HIGH).astype(jnp.bfloat16)
    new_basis, right_round = basis_part(row.astype(jnp.int32).reshape(1), inverse, blocks, other_blocks, units)
    new_error = weight_change.astype(jnp.float32) + error_buffer - dot(left_round, right_round, 0, 0)
    near, far_left, new_error = lax.optimization_barrier((near, far_left, new_error))
    other = lax.ppermute(near, "col", PAIR)
    halves = (BLOCKS, 2, R, LANES)
    slots = jnp.asarray(SLOTS, jnp.int32)[row]
    core = core.astype(jnp.int32).reshape(1)
    new_rollout = rollout(core, slots, far_left, near.reshape(halves), other.reshape(halves), weight)
    return (new_error, new_basis.T, new_rollout)


def solution(mesh):
    in_specs = (P("row", "col"), P("row", "col"), P("col", None), P("col", "row"))
    out_specs = (P("row", "col"), P("col", None), P("col", "row"))
    return jax.shard_map(local, mesh=mesh, in_specs=in_specs, out_specs=out_specs, check_vma=False)
```

```python
import jax
import jax.numpy as jnp
from jax import lax
from jax.experimental import pallas as pl
from jax.experimental.pallas import tpu as pltpu
from jax.sharding import PartitionSpec as P

HIGH = lax.Precision.HIGH
HIGHEST = lax.Precision.HIGHEST
ROWS, COLS, R, LANES, BLOCKS = 8, 32, 64, 128, 8
GRAM_END = R + R // 2
AXES = ("row", "col")


def row_hops(a, b):
    y = abs(a // 2 - b // 2)
    return min(y, 4 - y) + abs(a % 2 - b % 2)


def partners(row):
    rows = sorted(range(ROWS), key=lambda r: (row_hops(r, row), r))
    places = sorted(range(8), key=lambda k: (-min(k, 8 - k), k))
    return {r: (row + k) % 8 for r, k in zip(rows, places)}


SLOTS = [[partners(z)[r] for r in range(ROWS)] for z in range(8)]
SPREAD = [
    (r * COLS + 4 * z + q, z * COLS + 4 * SLOTS[z][r] + q)
    for r in range(ROWS)
    for z in range(8)
    for q in range(4)
]
SWAP = [(r * COLS + 4 * z + q, z * COLS + 4 * r + q) for r in range(ROWS) for z in range(8) for q in range(4)]
SAME_CORE = [
    [row * COLS + 4 * SLOTS[row][b] + 2 * half + core for b in range(ROWS) for half in range(2)]
    for row in range(ROWS)
    for core in range(2)
]
PAIR = [(c, c ^ 1) for c in range(COLS)]


def dot(a, b, ca, cb, precision=None):
    return lax.dot_general(
        a, b, (((ca,), (cb,)), ((), ())), precision=precision, preferred_element_type=jnp.float32
    )


def split(x):
    hi = x.astype(jnp.bfloat16)
    return hi, (x - hi.astype(jnp.float32)).astype(jnp.bfloat16)


def exchange(parts, axis, groups=None):
    return lax.all_to_all(parts, axis, 0, 0, axis_index_groups=groups)


ANY = pl.BlockSpec(memory_space=pl.ANY)
VMEM = pl.BlockSpec(memory_space=pltpu.VMEM)
SMEM = pl.BlockSpec(memory_space=pltpu.SMEM)


def grant(mib):
    return pltpu.CompilerParams(vmem_limit_bytes=mib * 2**20)


def left_kernel(change_ref, error_ref, basis_ref, out_ref, change_buf, error_buf, basis_buf, sem, basis_sem):
    rows, width = change_ref.shape[0], out_ref.shape[3]
    block = rows // 2
    basis_copy = pltpu.make_async_copy(basis_ref, basis_buf, basis_sem)
    basis_copy.start()
    copies = []
    for i in range(2):
        part = pl.ds(i * block, block)
        pair = [
            pltpu.make_async_copy(change_ref.at[part], change_buf.at[part], sem.at[0, i]),
            pltpu.make_async_copy(error_ref.at[part], error_buf.at[part], sem.at[1, i]),
        ]
        for copy in pair:
            copy.start()
        copies.append(pair)
    basis_copy.wait()
    basis_hi, basis_lo = split(basis_buf[...])
    basis_both = jnp.concatenate([basis_hi, basis_lo], 0)
    for i in range(2):
        for copy in copies[i]:
            copy.wait()
        part = pl.ds(i * block, block)
        hi, lo = split(change_buf[part].astype(jnp.float32) + error_buf[part])
        both = dot(basis_both, hi, 1, 1)
        left = both[:R] + both[R:] + dot(basis_hi, lo, 1, 1)
        for j in range(block // width):
            out_ref[:, i * (block // width) + j] = left[:, j * width : (j + 1) * width].reshape(8, 8, width)


def left_part(change, error, basis):
    rows, units = change.shape
    return pl.pallas_call(
        left_kernel,
        in_specs=[ANY, ANY, ANY],
        out_specs=VMEM,
        out_shape=jax.ShapeDtypeStruct((8, 4, 8, rows // 4), jnp.float32),
        scratch_shapes=[
            pltpu.VMEM((rows, units), jnp.bfloat16),
            pltpu.VMEM((rows, units), jnp.float32),
            pltpu.VMEM((R, units), jnp.float32),
            pltpu.SemaphoreType.DMA((2, 2)),
            pltpu.SemaphoreType.DMA,
        ],
        compiler_params=grant(62),
        cost_estimate=pl.CostEstimate(flops=6 * rows * units * R, bytes_accessed=6 * rows * units, transcendentals=0),
        name="left_part",
    )(change, error, basis)


def sum_share_kernel(parts_ref, out_ref):
    total = parts_ref[0]
    for i in range(1, parts_ref.shape[0]):
        total = total + parts_ref[i]
    for i in range(out_ref.shape[0]):
        out_ref[i] = total


def sum_share(parts):
    return pl.pallas_call(
        sum_share_kernel,
        in_specs=[VMEM],
        out_specs=VMEM,
        out_shape=jax.ShapeDtypeStruct(parts.shape, parts.dtype),
        compiler_params=grant(6),
        name="sum_share",
    )(parts)


def right_kernel(total_ref, left_ref, rows_ref, out_ref):
    left = jnp.concatenate([left_ref[:, i].reshape(R, -1) for i in range(4)], 1)
    both = dot(jnp.concatenate(split(left), 0), total_ref[...], 1, 0)
    right = both[:R] + both[R:]
    used = right.shape[1] // LANES
    for b in range(used):
        out_ref[b, :R] = right[:, b * LANES : (b + 1) * LANES]
    for b in range(used, BLOCKS):
        out_ref[b, :R] = jnp.zeros((R, LANES), jnp.float32)
    gram = dot(left, left, 1, 1, HIGHEST)
    for b in range(BLOCKS):
        out_ref[b, R : GRAM_END, :R] = gram[: R // 2]
        out_ref[b, R : GRAM_END, R:] = gram[R // 2 :]
        for i in range(rows_ref.shape[1] // LANES):
            out_ref[b, GRAM_END + 8 * i : GRAM_END + 8 * i + 8] = rows_ref[:, i * LANES : (i + 1) * LANES]


def right_part(total, left, some_rows):
    rows, units = total.shape
    return pl.pallas_call(
        right_kernel,
        in_specs=[VMEM, VMEM, VMEM],
        out_specs=VMEM,
        out_shape=jax.ShapeDtypeStruct((BLOCKS, GRAM_END + some_rows.size // LANES, LANES), jnp.float32),
        compiler_params=grant(12),
        cost_estimate=pl.CostEstimate(flops=4 * rows * units * R, bytes_accessed=2 * rows * units, transcendentals=0),
        name="right_part",
    )(total, left, some_rows)


def inverse_factor(gram):
    n = R // 8
    lane = lax.broadcasted_iota(jnp.int32, (8, R), 1)
    sub = lax.broadcasted_iota(jnp.int32, (8, R), 0)
    wide = [
        jnp.concatenate([gram[8 * i : 8 * i + 8], (lane == sub + 8 * i).astype(jnp.float32)], 1)
        for i in range(n)
    ]
    row = lax.broadcasted_iota(jnp.int32, (8, LANES), 0)
    out = []

    def pick(x, k):
        return jnp.broadcast_to(x[k : k + 1], (8, LANES))

    for p in range(n):
        column = [
            [jnp.broadcast_to(wide[i][:, 8 * p + k : 8 * p + k + 1], (8, LANES)) for i in range(p, n)]
            for k in range(8)
        ]
        scale = jnp.zeros((8, LANES), jnp.float32)
        for k in range(8):
            pivot = pick(column[k][0], k)
            times = 1.0 / pivot
            scale = jnp.where(row == k, lax.rsqrt(pivot), scale)
            by = [c * times for c in column[k]]
            by[0] = jnp.where(row > k, by[0], 0.0)
            for l in range(k + 1, 8):
                value = pick(column[l][0], k)
                column[l] = [c - b * value for c, b in zip(column[l], by)]
            value = pick(wide[p], k)
            for i in range(p, n):
                wide[i] = wide[i] - by[i - p] * value
        out.append(wide[p][:, R:] * scale[:, R:])
    return jnp.concatenate(out, 0)


def settle_kernel(parts_ref, block_ref, gram_ref, rows_ref):
    got = parts_ref[0, :GRAM_END]
    for b in range(1, BLOCKS):
        got = got + parts_ref[b, :GRAM_END]
    block_ref[...] = got[:R]
    gram_ref[...] = got[R:]
    for b in range(BLOCKS):
        for i in range(rows_ref.shape[1] // LANES):
            piece = parts_ref[b, GRAM_END + 8 * i : GRAM_END + 8 * i + 8]
            rows_ref[8 * b : 8 * b + 8, i * LANES : (i + 1) * LANES] = piece


def settle(parts):
    width = (parts.shape[1] - GRAM_END) // 8 * LANES
    return pl.pallas_call(
        settle_kernel,
        in_specs=[VMEM],
        out_specs=[VMEM, VMEM, VMEM],
        out_shape=[
            jax.ShapeDtypeStruct((R, LANES), jnp.float32),
            jax.ShapeDtypeStruct((R // 2, LANES), jnp.float32),
            jax.ShapeDtypeStruct((R, width), jnp.float32),
        ],
        compiler_params=grant(6),
        name="settle",
    )(parts)


def factor_kernel(gram_ref, block_ref, inverse_ref, copies_ref, same_ref):
    packed = gram_ref[...]
    same_ref[...] = block_ref[...]
    inverse = inverse_factor(jnp.concatenate([packed[:, :R], packed[:, R:]], 0))
    inverse_ref[...] = inverse
    for b in range(copies_ref.shape[0] // R):
        copies_ref[b * R : (b + 1) * R] = inverse


def factor(gram, block):
    return pl.pallas_call(
        factor_kernel,
        in_specs=[VMEM, VMEM],
        out_specs=[VMEM, VMEM, VMEM],
        out_shape=[
            jax.ShapeDtypeStruct((R, R), jnp.float32),
            jax.ShapeDtypeStruct((COLS // 2 * R, R), jnp.float32),
            jax.ShapeDtypeStruct((R, LANES), jnp.float32),
        ],
        compiler_params=grant(6),
        cost_estimate=pl.CostEstimate(flops=1, bytes_accessed=1, transcendentals=0),
        name="factor",
    )(gram, block)


def basis_kernel(row_ref, inverse_ref, mine_ref, other_ref, basis_ref, round_ref):
    y, odd = row_ref[0] // 2, row_ref[0] % 2
    blocks = []
    for b in range(basis_ref.shape[1] // LANES):
        value = jnp.zeros((R, LANES), jnp.float32)
        for k in range(4):
            lanes = slice(k * LANES, (k + 1) * LANES)
            picked = jnp.where(odd == b % 2, mine_ref[:, lanes], other_ref[:, lanes])
            value = jnp.where((y + 4 - k) % 4 == b // 2, picked, value)
        blocks.append(value)
    basis = dot(inverse_ref[...], jnp.concatenate(blocks, 1), 1, 0, HIGHEST)
    basis_ref[...] = basis
    round_ref[...] = basis.astype(jnp.bfloat16)


def basis_part(row, inverse, mine, other, units):
    return pl.pallas_call(
        basis_kernel,
        in_specs=[SMEM] + [VMEM] * 3,
        out_specs=[VMEM, VMEM],
        out_shape=[
            jax.ShapeDtypeStruct((R, units), jnp.float32),
            jax.ShapeDtypeStruct((R, units), jnp.bfloat16),
        ],
        compiler_params=grant(6),
        name="basis_part",
    )(row, inverse, mine, other)


def rollout_kernel(core_ref, left_ref, near_ref, other_ref, weight_ref, out_ref, buf, sem):
    even = core_ref[0] == 0
    width = buf.shape[2]
    copies = []
    for q in range(4):
        first, second = (near_ref, other_ref) if q % 2 == 0 else (other_ref, near_ref)
        blocks = [jnp.where(even, first[b, q // 2], second[b, q // 2]) for b in range(width // LANES)]
        delta = dot(left_ref[...], jnp.concatenate(blocks, 1), 1, 0)
        buf[q] = (weight_ref[q].astype(jnp.float32) + delta).astype(jnp.bfloat16)
        copy = pltpu.make_async_copy(buf.at[q], out_ref.at[:, pl.ds(q * width, width)], sem.at[q])
        copy.start()
        copies.append(copy)
    for copy in copies:
        copy.wait()


def rollout(core, left, near, other, weight):
    quarters, rows, width = weight.shape
    return pl.pallas_call(
        rollout_kernel,
        in_specs=[SMEM, VMEM, VMEM, VMEM, VMEM],
        out_specs=ANY,
        out_shape=jax.ShapeDtypeStruct((rows, quarters * width), jnp.bfloat16),
        scratch_shapes=[
            pltpu.VMEM((quarters, rows, width), jnp.bfloat16),
            pltpu.SemaphoreType.DMA((4,)),
        ],
        compiler_params=grant(12),
        name="rollout",
    )(core, left, near, other, weight)


def local(weight_change, error_buffer, basis, rollout_weight):
    row = lax.axis_index("row")
    core = lax.axis_index("col") % 2
    rows, units = weight_change.shape
    part = left_part(weight_change, error_buffer, basis.T)
    part, change, error = lax.optimization_barrier((part, weight_change, error_buffer))
    total = (change.astype(jnp.float32) + error).astype(jnp.bfloat16)
    parts = exchange(part.reshape(COLS, 8, rows // 4), "col")
    parts, total = lax.optimization_barrier((parts, total))
    chunks = sum_share(parts)
    some_rows = lax.ppermute(chunks[0], AXES, SWAP)
    left = exchange(chunks, "col").reshape(8, 4, 8, rows // 4)
    sums, weight = lax.optimization_barrier((right_part(total, left, some_rows), rollout_weight))
    weight = jnp.stack([weight[:, i * units : (i + 1) * units] for i in range(4)])
    parts, weight = lax.optimization_barrier((exchange(sums, "row"), weight))
    block, gram, far_left = settle(parts)
    far = lax.ppermute(block, AXES, SPREAD)
    inverse, copies, block = factor(gram, block)
    blocks = [lax.ppermute(block, "row", [(r, (r + 2 * k) % ROWS) for r in range(ROWS)]) for k in (1, 2, 3)]
    far_round = dot(copies, far, 1, 0, HIGH).astype(jnp.bfloat16).reshape(COLS // 2, R, LANES)
    far_round, inverse = lax.optimization_barrier((far_round, inverse))
    near = exchange(far_round, AXES, SAME_CORE)
    blocks = jnp.concatenate([block] + blocks, 1)
    other_blocks = lax.ppermute(blocks, "row", [(r, r ^ 1) for r in range(ROWS)])
    left_rows = left.transpose(0, 2, 1, 3).reshape(R, rows)
    left_round = dot(inverse, left_rows, 1, 0, HIGH).astype(jnp.bfloat16)
    far_left = dot(far_left, inverse, 0, 1, HIGH).astype(jnp.bfloat16)
    new_basis, right_round = basis_part(row.astype(jnp.int32).reshape(1), inverse, blocks, other_blocks, units)
    new_error = weight_change.astype(jnp.float32) + error_buffer - dot(left_round, right_round, 0, 0)
    near, far_left, new_error = lax.optimization_barrier((near, far_left, new_error))
    other = lax.ppermute(near, "col", PAIR)
    halves = (BLOCKS, 2, R, LANES)
    core = core.astype(jnp.int32).reshape(1)
    new_rollout = rollout(core, far_left, near.reshape(halves), other.reshape(halves), weight)
    return (new_error, new_basis.T, new_rollout)


def solution(mesh):
    in_specs = (P("row", "col"), P("row", "col"), P("col", None), P("col", "row"))
    out_specs = (P("row", "col"), P("col", None), P("col", "row"))
    return jax.shard_map(local, mesh=mesh, in_specs=in_specs, out_specs=out_specs, check_vma=False)
```

```python
import jax
import jax.numpy as jnp
from jax import lax
from jax.experimental import pallas as pl
from jax.experimental.pallas import tpu as pltpu
from jax.sharding import PartitionSpec as P

HIGH = lax.Precision.HIGH
HIGHEST = lax.Precision.HIGHEST
ROWS, COLS, R, LANES, BLOCKS = 8, 32, 64, 128, 8
GRAM_END = R + R // 2
AXES = ("row", "col")


def row_hops(a, b):
    y = abs(a // 2 - b // 2)
    return min(y, 4 - y) + abs(a % 2 - b % 2)


def partners(row):
    rows = sorted(range(ROWS), key=lambda r: (row_hops(r, row), r))
    places = sorted(range(8), key=lambda k: (-min(k, 8 - k), k))
    return {r: (row + k) % 8 for r, k in zip(rows, places)}


SLOTS = [[partners(z)[r] for r in range(ROWS)] for z in range(8)]
SPREAD = [
    (r * COLS + 4 * z + q, z * COLS + 4 * SLOTS[z][r] + q)
    for r in range(ROWS)
    for z in range(8)
    for q in range(4)
]
SWAP = [(r * COLS + 4 * z + q, z * COLS + 4 * r + q) for r in range(ROWS) for z in range(8) for q in range(4)]
SAME_CORE = [
    [row * COLS + 4 * SLOTS[row][b] + 2 * half + core for b in range(ROWS) for half in range(2)]
    for row in range(ROWS)
    for core in range(2)
]
PAIR = [(c, c ^ 1) for c in range(COLS)]


def dot(a, b, ca, cb, precision=None):
    return lax.dot_general(
        a, b, (((ca,), (cb,)), ((), ())), precision=precision, preferred_element_type=jnp.float32
    )


def split(x):
    hi = x.astype(jnp.bfloat16)
    return hi, (x - hi.astype(jnp.float32)).astype(jnp.bfloat16)


def exchange(parts, axis, groups=None):
    return lax.all_to_all(parts, axis, 0, 0, axis_index_groups=groups)


ANY = pl.BlockSpec(memory_space=pl.ANY)
VMEM = pl.BlockSpec(memory_space=pltpu.VMEM)
SMEM = pl.BlockSpec(memory_space=pltpu.SMEM)


def grant(mib):
    return pltpu.CompilerParams(vmem_limit_bytes=mib * 2**20)


def left_kernel(change_ref, error_ref, basis_ref, out_ref, change_buf, error_buf, basis_buf, sem, basis_sem):
    rows, width = change_ref.shape[0], out_ref.shape[3]
    block = rows // 2
    basis_copy = pltpu.make_async_copy(basis_ref, basis_buf, basis_sem)
    basis_copy.start()
    copies = []
    for i in range(2):
        part = pl.ds(i * block, block)
        pair = [
            pltpu.make_async_copy(change_ref.at[part], change_buf.at[part], sem.at[0, i]),
            pltpu.make_async_copy(error_ref.at[part], error_buf.at[part], sem.at[1, i]),
        ]
        for copy in pair:
            copy.start()
        copies.append(pair)
    basis_copy.wait()
    basis_hi, basis_lo = split(basis_buf[...])
    basis_both = jnp.concatenate([basis_hi, basis_lo], 0)
    for i in range(2):
        for copy in copies[i]:
            copy.wait()
        part = pl.ds(i * block, block)
        hi, lo = split(change_buf[part].astype(jnp.float32) + error_buf[part])
        both = dot(basis_both, hi, 1, 1)
        left = both[:R] + both[R:] + dot(basis_hi, lo, 1, 1)
        for j in range(block // width):
            out_ref[:, i * (block // width) + j] = left[:, j * width : (j + 1) * width].reshape(8, 8, width)


def left_part(change, error, basis):
    rows, units = change.shape
    return pl.pallas_call(
        left_kernel,
        in_specs=[ANY, ANY, ANY],
        out_specs=VMEM,
        out_shape=jax.ShapeDtypeStruct((8, 4, 8, rows // 4), jnp.float32),
        scratch_shapes=[
            pltpu.VMEM((rows, units), jnp.bfloat16),
            pltpu.VMEM((rows, units), jnp.float32),
            pltpu.VMEM((R, units), jnp.float32),
            pltpu.SemaphoreType.DMA((2, 2)),
            pltpu.SemaphoreType.DMA,
        ],
        compiler_params=grant(62),
        cost_estimate=pl.CostEstimate(flops=6 * rows * units * R, bytes_accessed=6 * rows * units, transcendentals=0),
        name="left_part",
    )(change, error, basis)


def sum_share_kernel(parts_ref, out_ref):
    total = parts_ref[0]
    for i in range(1, parts_ref.shape[0]):
        total = total + parts_ref[i]
    for i in range(out_ref.shape[0]):
        out_ref[i] = total


def sum_share(parts):
    return pl.pallas_call(
        sum_share_kernel,
        in_specs=[VMEM],
        out_specs=VMEM,
        out_shape=jax.ShapeDtypeStruct(parts.shape, parts.dtype),
        compiler_params=grant(6),
        name="sum_share",
    )(parts)


def right_kernel(total_ref, left_ref, rows_ref, out_ref):
    left = jnp.concatenate([left_ref[:, i].reshape(R, -1) for i in range(4)], 1)
    both = dot(jnp.concatenate(split(left), 0), total_ref[...], 1, 0)
    right = both[:R] + both[R:]
    used = right.shape[1] // LANES
    for b in range(used):
        out_ref[b, :R] = right[:, b * LANES : (b + 1) * LANES]
    for b in range(used, BLOCKS):
        out_ref[b, :R] = jnp.zeros((R, LANES), jnp.float32)
    gram = dot(left, left, 1, 1, HIGHEST)
    for b in range(BLOCKS):
        out_ref[b, R : GRAM_END, :R] = gram[: R // 2]
        out_ref[b, R : GRAM_END, R:] = gram[R // 2 :]
        for i in range(rows_ref.shape[1] // LANES):
            out_ref[b, GRAM_END + 8 * i : GRAM_END + 8 * i + 8] = rows_ref[:, i * LANES : (i + 1) * LANES]


def right_part(total, left, some_rows):
    rows, units = total.shape
    return pl.pallas_call(
        right_kernel,
        in_specs=[VMEM, VMEM, VMEM],
        out_specs=VMEM,
        out_shape=jax.ShapeDtypeStruct((BLOCKS, GRAM_END + some_rows.size // LANES, LANES), jnp.float32),
        compiler_params=grant(12),
        cost_estimate=pl.CostEstimate(flops=4 * rows * units * R, bytes_accessed=2 * rows * units, transcendentals=0),
        name="right_part",
    )(total, left, some_rows)


def inverse_factor(gram):
    n = R // 8
    lane = lax.broadcasted_iota(jnp.int32, (8, R), 1)
    sub = lax.broadcasted_iota(jnp.int32, (8, R), 0)
    wide = [
        jnp.concatenate([gram[8 * i : 8 * i + 8], (lane == sub + 8 * i).astype(jnp.float32)], 1)
        for i in range(n)
    ]
    row = lax.broadcasted_iota(jnp.int32, (8, LANES), 0)
    out = []

    def pick(x, k):
        return jnp.broadcast_to(x[k : k + 1], (8, LANES))

    for p in range(n):
        column = [
            [jnp.broadcast_to(wide[i][:, 8 * p + k : 8 * p + k + 1], (8, LANES)) for i in range(p, n)]
            for k in range(8)
        ]
        scale = jnp.zeros((8, LANES), jnp.float32)
        for k in range(8):
            pivot = pick(column[k][0], k)
            times = 1.0 / pivot
            scale = jnp.where(row == k, lax.rsqrt(pivot), scale)
            by = [c * times for c in column[k]]
            by[0] = jnp.where(row > k, by[0], 0.0)
            for l in range(k + 1, 8):
                value = pick(column[l][0], k)
                column[l] = [c - b * value for c, b in zip(column[l], by)]
            value = pick(wide[p], k)
            for i in range(p, n):
                wide[i] = wide[i] - by[i - p] * value
        out.append(wide[p][:, R:] * scale[:, R:])
    return jnp.concatenate(out, 0)


def settle_kernel(parts_ref, block_ref, gram_ref, rows_ref):
    got = parts_ref[0, :GRAM_END]
    for b in range(1, BLOCKS):
        got = got + parts_ref[b, :GRAM_END]
    block_ref[...] = got[:R]
    gram_ref[...] = got[R:]
    for b in range(BLOCKS):
        for i in range(rows_ref.shape[1] // LANES):
            piece = parts_ref[b, GRAM_END + 8 * i : GRAM_END + 8 * i + 8]
            rows_ref[8 * b : 8 * b + 8, i * LANES : (i + 1) * LANES] = piece


def settle(parts):
    width = (parts.shape[1] - GRAM_END) // 8 * LANES
    return pl.pallas_call(
        settle_kernel,
        in_specs=[VMEM],
        out_specs=[VMEM, VMEM, VMEM],
        out_shape=[
            jax.ShapeDtypeStruct((R, LANES), jnp.float32),
            jax.ShapeDtypeStruct((R // 2, LANES), jnp.float32),
            jax.ShapeDtypeStruct((R, width), jnp.float32),
        ],
        compiler_params=grant(6),
        name="settle",
    )(parts)


def factor_kernel(gram_ref, inverse_ref, copies_ref):
    packed = gram_ref[...]
    inverse = inverse_factor(jnp.concatenate([packed[:, :R], packed[:, R:]], 0))
    inverse_ref[...] = inverse
    for b in range(copies_ref.shape[0] // R):
        copies_ref[b * R : (b + 1) * R] = inverse


def factor(gram):
    return pl.pallas_call(
        factor_kernel,
        in_specs=[VMEM],
        out_specs=[VMEM, VMEM],
        out_shape=[
            jax.ShapeDtypeStruct((R, R), jnp.float32),
            jax.ShapeDtypeStruct((COLS // 2 * R, R), jnp.float32),
        ],
        compiler_params=grant(6),
        cost_estimate=pl.CostEstimate(flops=1, bytes_accessed=1, transcendentals=0),
        name="factor",
    )(gram)


def basis_kernel(row_ref, inverse_ref, pair0_ref, pair1_ref, pair2_ref, pair3_ref, basis_ref, round_ref):
    y = row_ref[0] // 2
    blocks = []
    for b in range(basis_ref.shape[1] // LANES):
        lanes = slice(b % 2 * LANES, (b % 2 + 1) * LANES)
        value = pair0_ref[:, lanes]
        for k, ref in enumerate((pair1_ref, pair2_ref, pair3_ref), 1):
            value = jnp.where((y + 4 - k) % 4 == b // 2, ref[:, lanes], value)
        blocks.append(value)
    basis = dot(inverse_ref[...], jnp.concatenate(blocks, 1), 1, 0, HIGHEST)
    basis_ref[...] = basis
    round_ref[...] = basis.astype(jnp.bfloat16)


def basis_part(row, inverse, pairs, units):
    return pl.pallas_call(
        basis_kernel,
        in_specs=[SMEM] + [VMEM] * 5,
        out_specs=[VMEM, VMEM],
        out_shape=[
            jax.ShapeDtypeStruct((R, units), jnp.float32),
            jax.ShapeDtypeStruct((R, units), jnp.bfloat16),
        ],
        compiler_params=grant(6),
        name="basis_part",
    )(row, inverse, *pairs)


def rollout_kernel(core_ref, left_ref, near_ref, other_ref, weight_ref, out_ref, buf, sem):
    even = core_ref[0] == 0
    width = buf.shape[2]
    copies = []
    for q in range(4):
        first, second = (near_ref, other_ref) if q % 2 == 0 else (other_ref, near_ref)
        blocks = [jnp.where(even, first[b, q // 2], second[b, q // 2]) for b in range(width // LANES)]
        delta = dot(left_ref[...], jnp.concatenate(blocks, 1), 1, 0)
        buf[q] = (weight_ref[q].astype(jnp.float32) + delta).astype(jnp.bfloat16)
        copy = pltpu.make_async_copy(buf.at[q], out_ref.at[:, pl.ds(q * width, width)], sem.at[q])
        copy.start()
        copies.append(copy)
    for copy in copies:
        copy.wait()


def rollout(core, left, near, other, weight):
    quarters, rows, width = weight.shape
    return pl.pallas_call(
        rollout_kernel,
        in_specs=[SMEM, VMEM, VMEM, VMEM, VMEM],
        out_specs=ANY,
        out_shape=jax.ShapeDtypeStruct((rows, quarters * width), jnp.bfloat16),
        scratch_shapes=[
            pltpu.VMEM((quarters, rows, width), jnp.bfloat16),
            pltpu.SemaphoreType.DMA((4,)),
        ],
        compiler_params=grant(12),
        name="rollout",
    )(core, left, near, other, weight)


def local(weight_change, error_buffer, basis, rollout_weight):
    row = lax.axis_index("row")
    core = lax.axis_index("col") % 2
    rows, units = weight_change.shape
    part = left_part(weight_change, error_buffer, basis.T)
    part, change, error = lax.optimization_barrier((part, weight_change, error_buffer))
    total = (change.astype(jnp.float32) + error).astype(jnp.bfloat16)
    parts = exchange(part.reshape(COLS, 8, rows // 4), "col")
    parts, total = lax.optimization_barrier((parts, total))
    chunks = sum_share(parts)
    some_rows = lax.ppermute(chunks[0], AXES, SWAP)
    left = exchange(chunks, "col").reshape(8, 4, 8, rows // 4)
    parts = exchange(right_part(total, left, some_rows), "row")
    block, gram, far_left = settle(parts)
    far = lax.ppermute(block, AXES, SPREAD)
    other_block = lax.ppermute(block, "row", [(r, r ^ 1) for r in range(ROWS)])
    inverse, copies = factor(gram)
    odd = row % 2 == 1
    pair = jnp.concatenate([jnp.where(odd, other_block, block), jnp.where(odd, block, other_block)], 1)
    pairs = [lax.ppermute(pair, "row", [(r, (r + 2 * k) % ROWS) for r in range(ROWS)]) for k in (1, 2, 3)]
    far_round = dot(copies, far, 1, 0, HIGH).astype(jnp.bfloat16).reshape(COLS // 2, R, LANES)
    far_round, inverse, weight = lax.optimization_barrier((far_round, inverse, rollout_weight))
    near = exchange(far_round, AXES, SAME_CORE)
    weight = jnp.stack([weight[:, i * units : (i + 1) * units] for i in range(4)])
    left_rows = left.transpose(0, 2, 1, 3).reshape(R, rows)
    left_round = dot(inverse, left_rows, 1, 0, HIGH).astype(jnp.bfloat16)
    far_left = dot(far_left, inverse, 0, 1, HIGH).astype(jnp.bfloat16)
    new_basis, right_round = basis_part(row.astype(jnp.int32).reshape(1), inverse, [pair] + pairs, units)
    new_error = weight_change.astype(jnp.float32) + error_buffer - dot(left_round, right_round, 0, 0)
    near, far_left, new_error, weight = lax.optimization_barrier((near, far_left, new_error, weight))
    other = lax.ppermute(near, "col", PAIR)
    halves = (BLOCKS, 2, R, LANES)
    core = core.astype(jnp.int32).reshape(1)
    new_rollout = rollout(core, far_left, near.reshape(halves), other.reshape(halves), weight)
    return (new_error, new_basis.T, new_rollout)


def solution(mesh):
    in_specs = (P("row", "col"), P("row", "col"), P("col", None), P("col", "row"))
    out_specs = (P("row", "col"), P("col", None), P("col", "row"))
    return jax.shard_map(local, mesh=mesh, in_specs=in_specs, out_specs=out_specs, check_vma=False)
```

```python
import jax
import jax.numpy as jnp
from jax import lax
from jax.experimental import pallas as pl
from jax.experimental.pallas import tpu as pltpu
from jax.sharding import PartitionSpec as P

HIGH = lax.Precision.HIGH
HIGHEST = lax.Precision.HIGHEST
ROWS, COLS, R, LANES, BLOCKS = 8, 32, 64, 128, 8
GRAM_END = R + R // 2
AXES = ("row", "col")


def row_hops(a, b):
    y = abs(a // 2 - b // 2)
    return min(y, 4 - y) + abs(a % 2 - b % 2)


def partners(row):
    rows = sorted(range(ROWS), key=lambda r: (row_hops(r, row), r))
    places = sorted(range(8), key=lambda k: (-min(k, 8 - k), k))
    return {r: (row + k) % 8 for r, k in zip(rows, places)}


SLOTS = [[partners(z)[r] for r in range(ROWS)] for z in range(8)]
SPREAD = [
    (r * COLS + 4 * z + q, z * COLS + 4 * SLOTS[z][r] + q)
    for r in range(ROWS)
    for z in range(8)
    for q in range(4)
]
FANOUT = [
    (r * COLS + 4 * z + q, t * COLS + 4 * r + q)
    for r in range(ROWS)
    for t, z in partners(r).items()
    for q in range(4)
]
SAME_CORE = [
    [row * COLS + 4 * SLOTS[row][b] + 2 * half + core for b in range(ROWS) for half in range(2)]
    for row in range(ROWS)
    for core in range(2)
]
PAIR = [(c, c ^ 1) for c in range(COLS)]


def dot(a, b, ca, cb, precision=None):
    return lax.dot_general(
        a, b, (((ca,), (cb,)), ((), ())), precision=precision, preferred_element_type=jnp.float32
    )


def split(x):
    hi = x.astype(jnp.bfloat16)
    return hi, (x - hi.astype(jnp.float32)).astype(jnp.bfloat16)


def exchange(parts, axis, groups=None):
    return lax.all_to_all(parts, axis, 0, 0, axis_index_groups=groups)


ANY = pl.BlockSpec(memory_space=pl.ANY)
VMEM = pl.BlockSpec(memory_space=pltpu.VMEM)
SMEM = pl.BlockSpec(memory_space=pltpu.SMEM)


def grant(mib):
    return pltpu.CompilerParams(vmem_limit_bytes=mib * 2**20)


def left_kernel(change_ref, error_ref, basis_ref, out_ref, change_buf, error_buf, basis_buf, sem, basis_sem):
    rows, width = change_ref.shape[0], out_ref.shape[3]
    block = rows // 2
    basis_copy = pltpu.make_async_copy(basis_ref, basis_buf, basis_sem)
    basis_copy.start()
    copies = []
    for i in range(2):
        part = pl.ds(i * block, block)
        pair = [
            pltpu.make_async_copy(change_ref.at[part], change_buf.at[part], sem.at[0, i]),
            pltpu.make_async_copy(error_ref.at[part], error_buf.at[part], sem.at[1, i]),
        ]
        for copy in pair:
            copy.start()
        copies.append(pair)
    basis_copy.wait()
    basis_hi, basis_lo = split(basis_buf[...])
    basis_both = jnp.concatenate([basis_hi, basis_lo], 0)
    for i in range(2):
        for copy in copies[i]:
            copy.wait()
        part = pl.ds(i * block, block)
        hi, lo = split(change_buf[part].astype(jnp.float32) + error_buf[part])
        both = dot(basis_both, hi, 1, 1)
        left = both[:R] + both[R:] + dot(basis_hi, lo, 1, 1)
        for j in range(block // width):
            out_ref[:, i * (block // width) + j] = left[:, j * width : (j + 1) * width].reshape(8, 8, width)


def left_part(change, error, basis):
    rows, units = change.shape
    return pl.pallas_call(
        left_kernel,
        in_specs=[ANY, ANY, ANY],
        out_specs=VMEM,
        out_shape=jax.ShapeDtypeStruct((8, 4, 8, rows // 4), jnp.float32),
        scratch_shapes=[
            pltpu.VMEM((rows, units), jnp.bfloat16),
            pltpu.VMEM((rows, units), jnp.float32),
            pltpu.VMEM((R, units), jnp.float32),
            pltpu.SemaphoreType.DMA((2, 2)),
            pltpu.SemaphoreType.DMA,
        ],
        compiler_params=grant(62),
        cost_estimate=pl.CostEstimate(flops=6 * rows * units * R, bytes_accessed=6 * rows * units, transcendentals=0),
        name="left_part",
    )(change, error, basis)


def sum_share_kernel(parts_ref, out_ref):
    total = parts_ref[0]
    for i in range(1, parts_ref.shape[0]):
        total = total + parts_ref[i]
    for i in range(out_ref.shape[0]):
        out_ref[i] = total


def sum_share(parts):
    return pl.pallas_call(
        sum_share_kernel,
        in_specs=[VMEM],
        out_specs=VMEM,
        out_shape=jax.ShapeDtypeStruct(parts.shape, parts.dtype),
        compiler_params=grant(6),
        name="sum_share",
    )(parts)


def right_kernel(total_ref, left_ref, out_ref):
    left = jnp.concatenate([left_ref[:, i].reshape(R, -1) for i in range(4)], 1)
    both = dot(jnp.concatenate(split(left), 0), total_ref[...], 1, 0)
    right = both[:R] + both[R:]
    used = right.shape[1] // LANES
    for b in range(used):
        out_ref[b, :R] = right[:, b * LANES : (b + 1) * LANES]
    for b in range(used, BLOCKS):
        out_ref[b, :R] = jnp.zeros((R, LANES), jnp.float32)
    gram = dot(left, left, 1, 1, HIGHEST)
    for b in range(BLOCKS):
        out_ref[b, R : GRAM_END, :R] = gram[: R // 2]
        out_ref[b, R : GRAM_END, R:] = gram[R // 2 :]


def right_part(total, left):
    rows, units = total.shape
    return pl.pallas_call(
        right_kernel,
        in_specs=[VMEM, VMEM],
        out_specs=VMEM,
        out_shape=jax.ShapeDtypeStruct((BLOCKS, GRAM_END, LANES), jnp.float32),
        compiler_params=grant(12),
        cost_estimate=pl.CostEstimate(flops=4 * rows * units * R, bytes_accessed=2 * rows * units, transcendentals=0),
        name="right_part",
    )(total, left)


def inverse_factor(gram):
    n = R // 8
    lane = lax.broadcasted_iota(jnp.int32, (8, R), 1)
    sub = lax.broadcasted_iota(jnp.int32, (8, R), 0)
    wide = [
        jnp.concatenate([gram[8 * i : 8 * i + 8], (lane == sub + 8 * i).astype(jnp.float32)], 1)
        for i in range(n)
    ]
    row = lax.broadcasted_iota(jnp.int32, (8, LANES), 0)
    out = []

    def pick(x, k):
        return jnp.broadcast_to(x[k : k + 1], (8, LANES))

    for p in range(n):
        column = [
            [jnp.broadcast_to(wide[i][:, 8 * p + k : 8 * p + k + 1], (8, LANES)) for i in range(p, n)]
            for k in range(8)
        ]
        scale = jnp.zeros((8, LANES), jnp.float32)
        for k in range(8):
            pivot = pick(column[k][0], k)
            times = 1.0 / pivot
            scale = jnp.where(row == k, lax.rsqrt(pivot), scale)
            by = [c * times for c in column[k]]
            by[0] = jnp.where(row > k, by[0], 0.0)
            for l in range(k + 1, 8):
                value = pick(column[l][0], k)
                column[l] = [c - b * value for c, b in zip(column[l], by)]
            value = pick(wide[p], k)
            for i in range(p, n):
                wide[i] = wide[i] - by[i - p] * value
        out.append(wide[p][:, R:] * scale[:, R:])
    return jnp.concatenate(out, 0)


def settle_kernel(parts_ref, block_ref, gram_ref):
    got = parts_ref[0]
    for b in range(1, BLOCKS):
        got = got + parts_ref[b]
    block_ref[...] = got[:R]
    gram_ref[...] = got[R:]


def settle(parts):
    return pl.pallas_call(
        settle_kernel,
        in_specs=[VMEM],
        out_specs=[VMEM, VMEM],
        out_shape=[
            jax.ShapeDtypeStruct((R, LANES), jnp.float32),
            jax.ShapeDtypeStruct((R // 2, LANES), jnp.float32),
        ],
        compiler_params=grant(6),
        name="settle",
    )(parts)


def factor_kernel(gram_ref, inverse_ref, copies_ref):
    packed = gram_ref[...]
    inverse = inverse_factor(jnp.concatenate([packed[:, :R], packed[:, R:]], 0))
    inverse_ref[...] = inverse
    for b in range(copies_ref.shape[0] // R):
        copies_ref[b * R : (b + 1) * R] = inverse


def factor(gram):
    return pl.pallas_call(
        factor_kernel,
        in_specs=[VMEM],
        out_specs=[VMEM, VMEM],
        out_shape=[
            jax.ShapeDtypeStruct((R, R), jnp.float32),
            jax.ShapeDtypeStruct((COLS // 2 * R, R), jnp.float32),
        ],
        compiler_params=grant(6),
        cost_estimate=pl.CostEstimate(flops=1, bytes_accessed=1, transcendentals=0),
        name="factor",
    )(gram)


def basis_kernel(row_ref, inverse_ref, pair0_ref, pair1_ref, pair2_ref, pair3_ref, basis_ref, round_ref):
    y = row_ref[0] // 2
    blocks = []
    for b in range(basis_ref.shape[1] // LANES):
        lanes = slice(b % 2 * LANES, (b % 2 + 1) * LANES)
        value = pair0_ref[:, lanes]
        for k, ref in enumerate((pair1_ref, pair2_ref, pair3_ref), 1):
            value = jnp.where((y + 4 - k) % 4 == b // 2, ref[:, lanes], value)
        blocks.append(value)
    basis = dot(inverse_ref[...], jnp.concatenate(blocks, 1), 1, 0, HIGHEST)
    basis_ref[...] = basis
    round_ref[...] = basis.astype(jnp.bfloat16)


def basis_part(row, inverse, pairs, units):
    return pl.pallas_call(
        basis_kernel,
        in_specs=[SMEM] + [VMEM] * 5,
        out_specs=[VMEM, VMEM],
        out_shape=[
            jax.ShapeDtypeStruct((R, units), jnp.float32),
            jax.ShapeDtypeStruct((R, units), jnp.bfloat16),
        ],
        compiler_params=grant(6),
        name="basis_part",
    )(row, inverse, *pairs)


def rollout_kernel(core_ref, left_ref, near_ref, other_ref, weight_ref, out_ref, buf, sem):
    even = core_ref[0] == 0
    width = buf.shape[2]
    copies = []
    for q in range(4):
        first, second = (near_ref, other_ref) if q % 2 == 0 else (other_ref, near_ref)
        blocks = [jnp.where(even, first[b, q // 2], second[b, q // 2]) for b in range(width // LANES)]
        delta = dot(left_ref[...], jnp.concatenate(blocks, 1), 0, 0)
        buf[q] = (weight_ref[q].astype(jnp.float32) + delta).astype(jnp.bfloat16)
        copy = pltpu.make_async_copy(buf.at[q], out_ref.at[:, pl.ds(q * width, width)], sem.at[q])
        copy.start()
        copies.append(copy)
    for copy in copies:
        copy.wait()


def rollout(core, left, near, other, weight):
    quarters, rows, width = weight.shape
    return pl.pallas_call(
        rollout_kernel,
        in_specs=[SMEM, VMEM, VMEM, VMEM, VMEM],
        out_specs=ANY,
        out_shape=jax.ShapeDtypeStruct((rows, quarters * width), jnp.bfloat16),
        scratch_shapes=[
            pltpu.VMEM((quarters, rows, width), jnp.bfloat16),
            pltpu.SemaphoreType.DMA((4,)),
        ],
        compiler_params=grant(12),
        name="rollout",
    )(core, left, near, other, weight)


def local(weight_change, error_buffer, basis, rollout_weight):
    row = lax.axis_index("row")
    q = lax.axis_index("col") % 4
    rows, units = weight_change.shape
    part = left_part(weight_change, error_buffer, basis.T)
    part, change, error = lax.optimization_barrier((part, weight_change, error_buffer))
    total = (change.astype(jnp.float32) + error).astype(jnp.bfloat16)
    parts = exchange(part.reshape(COLS, 8, rows // 4), "col")
    parts, total = lax.optimization_barrier((parts, total))
    left = exchange(sum_share(parts), "col").reshape(8, 4, 8, rows // 4)
    block, gram = settle(exchange(right_part(total, left), "row"))
    far = lax.ppermute(block, AXES, SPREAD)
    other_block = lax.ppermute(block, "row", [(r, r ^ 1) for r in range(ROWS)])
    inverse, copies = factor(gram)
    odd = row % 2 == 1
    pair = jnp.concatenate([jnp.where(odd, other_block, block), jnp.where(odd, block, other_block)], 1)
    pairs = [lax.ppermute(pair, "row", [(r, (r + 2 * k) % ROWS) for r in range(ROWS)]) for k in (1, 2, 3)]
    far_round = dot(copies, far, 1, 0, HIGH).astype(jnp.bfloat16).reshape(COLS // 2, R, LANES)
    mine = lax.dynamic_index_in_dim(left, q, 1, keepdims=False).reshape(R, rows // 4)
    far_round, inverse, weight, mine = lax.optimization_barrier((far_round, inverse, rollout_weight, mine))
    far_left = lax.ppermute(dot(inverse, mine, 1, 0, HIGH).astype(jnp.bfloat16), AXES, FANOUT)
    near = exchange(far_round, AXES, SAME_CORE)
    weight = jnp.stack([weight[:, i * units : (i + 1) * units] for i in range(4)])
    left_rows = left.transpose(0, 2, 1, 3).reshape(R, rows)
    left_round = dot(inverse, left_rows, 1, 0, HIGH).astype(jnp.bfloat16)
    new_basis, right_round = basis_part(row.astype(jnp.int32).reshape(1), inverse, [pair] + pairs, units)
    new_error = weight_change.astype(jnp.float32) + error_buffer - dot(left_round, right_round, 0, 0)
    near, new_error, weight, far_left = lax.optimization_barrier((near, new_error, weight, far_left))
    other = lax.ppermute(near, "col", PAIR)
    halves = (BLOCKS, 2, R, LANES)
    core = (q % 2).astype(jnp.int32).reshape(1)
    new_rollout = rollout(core, far_left, near.reshape(halves), other.reshape(halves), weight)
    return (new_error, new_basis.T, new_rollout)


def solution(mesh):
    in_specs = (P("row", "col"), P("row", "col"), P("col", None), P("col", "row"))
    out_specs = (P("row", "col"), P("col", None), P("col", "row"))
    return jax.shard_map(local, mesh=mesh, in_specs=in_specs, out_specs=out_specs, check_vma=False)
```

```python
import jax
import jax.numpy as jnp
from jax import lax
from jax.experimental import pallas as pl
from jax.experimental.pallas import tpu as pltpu
from jax.sharding import PartitionSpec as P

HIGH = lax.Precision.HIGH
HIGHEST = lax.Precision.HIGHEST
ROWS, COLS, R, LANES, BLOCKS = 8, 32, 64, 128, 8
GRAM_END = R + R // 2
AXES = ("row", "col")


def row_hops(a, b):
    y = abs(a // 2 - b // 2)
    return min(y, 4 - y) + abs(a % 2 - b % 2)


def partners(row):
    rows = sorted(range(ROWS), key=lambda r: (row_hops(r, row), r))
    places = sorted(range(8), key=lambda k: (-min(k, 8 - k), k))
    return {r: (row + k) % 8 for r, k in zip(rows, places)}


SLOTS = [[partners(z)[r] for r in range(ROWS)] for z in range(8)]
SPREAD = [
    (r * COLS + 4 * z + q, z * COLS + 4 * SLOTS[z][r] + q)
    for r in range(ROWS)
    for z in range(8)
    for q in range(4)
]
FANOUT = [
    (r * COLS + 4 * z + q, t * COLS + 4 * r + q)
    for r in range(ROWS)
    for t, z in partners(r).items()
    for q in range(4)
]
SAME_CORE = [
    [row * COLS + 4 * SLOTS[row][b] + 2 * half + core for b in range(ROWS) for half in range(2)]
    for row in range(ROWS)
    for core in range(2)
]
PAIR = [(c, c ^ 1) for c in range(COLS)]


def dot(a, b, ca, cb, precision=None):
    return lax.dot_general(
        a, b, (((ca,), (cb,)), ((), ())), precision=precision, preferred_element_type=jnp.float32
    )


def split(x):
    hi = x.astype(jnp.bfloat16)
    return hi, (x - hi.astype(jnp.float32)).astype(jnp.bfloat16)


def exchange(parts, axis, groups=None):
    return lax.all_to_all(parts, axis, 0, 0, axis_index_groups=groups)


ANY = pl.BlockSpec(memory_space=pl.ANY)
VMEM = pl.BlockSpec(memory_space=pltpu.VMEM)
SMEM = pl.BlockSpec(memory_space=pltpu.SMEM)


def grant(mib):
    return pltpu.CompilerParams(vmem_limit_bytes=mib * 2**20)


def left_kernel(change_ref, error_ref, basis_ref, out_ref, change_buf, error_buf, basis_buf, sem, basis_sem):
    rows, width = change_ref.shape[0], out_ref.shape[3]
    block = rows // 2
    basis_copy = pltpu.make_async_copy(basis_ref, basis_buf, basis_sem)
    basis_copy.start()
    copies = []
    for i in range(2):
        part = pl.ds(i * block, block)
        pair = [
            pltpu.make_async_copy(change_ref.at[part], change_buf.at[part], sem.at[0, i]),
            pltpu.make_async_copy(error_ref.at[part], error_buf.at[part], sem.at[1, i]),
        ]
        for copy in pair:
            copy.start()
        copies.append(pair)
    basis_copy.wait()
    basis_hi, basis_lo = split(basis_buf[...])
    basis_both = jnp.concatenate([basis_hi, basis_lo], 0)
    for i in range(2):
        for copy in copies[i]:
            copy.wait()
        part = pl.ds(i * block, block)
        hi, lo = split(change_buf[part].astype(jnp.float32) + error_buf[part])
        both = dot(basis_both, hi, 1, 1)
        left = both[:R] + both[R:] + dot(basis_hi, lo, 1, 1)
        for j in range(block // width):
            out_ref[:, i * (block // width) + j] = left[:, j * width : (j + 1) * width].reshape(8, 8, width)


def left_part(change, error, basis):
    rows, units = change.shape
    return pl.pallas_call(
        left_kernel,
        in_specs=[ANY, ANY, ANY],
        out_specs=VMEM,
        out_shape=jax.ShapeDtypeStruct((8, 4, 8, rows // 4), jnp.float32),
        scratch_shapes=[
            pltpu.VMEM((rows, units), jnp.bfloat16),
            pltpu.VMEM((rows, units), jnp.float32),
            pltpu.VMEM((R, units), jnp.float32),
            pltpu.SemaphoreType.DMA((2, 2)),
            pltpu.SemaphoreType.DMA,
        ],
        compiler_params=grant(62),
        cost_estimate=pl.CostEstimate(flops=6 * rows * units * R, bytes_accessed=6 * rows * units, transcendentals=0),
        name="left_part",
    )(change, error, basis)


def sum_share_kernel(parts_ref, out_ref):
    total = parts_ref[0]
    for i in range(1, parts_ref.shape[0]):
        total = total + parts_ref[i]
    for i in range(out_ref.shape[0]):
        out_ref[i] = total


def sum_share(parts):
    return pl.pallas_call(
        sum_share_kernel,
        in_specs=[VMEM],
        out_specs=VMEM,
        out_shape=jax.ShapeDtypeStruct(parts.shape, parts.dtype),
        compiler_params=grant(6),
        name="sum_share",
    )(parts)


def right_kernel(total_ref, left_ref, out_ref):
    left = jnp.concatenate([left_ref[:, i].reshape(R, -1) for i in range(4)], 1)
    both = dot(jnp.concatenate(split(left), 0), total_ref[...], 1, 0)
    right = both[:R] + both[R:]
    used = right.shape[1] // LANES
    for b in range(used):
        out_ref[b, :R] = right[:, b * LANES : (b + 1) * LANES]
    for b in range(used, BLOCKS):
        out_ref[b, :R] = jnp.zeros((R, LANES), jnp.float32)
    gram = dot(left, left, 1, 1, HIGHEST)
    for b in range(BLOCKS):
        out_ref[b, R : GRAM_END, :R] = gram[: R // 2]
        out_ref[b, R : GRAM_END, R:] = gram[R // 2 :]


def right_part(total, left):
    rows, units = total.shape
    return pl.pallas_call(
        right_kernel,
        in_specs=[VMEM, VMEM],
        out_specs=VMEM,
        out_shape=jax.ShapeDtypeStruct((BLOCKS, GRAM_END, LANES), jnp.float32),
        compiler_params=grant(12),
        cost_estimate=pl.CostEstimate(flops=4 * rows * units * R, bytes_accessed=2 * rows * units, transcendentals=0),
        name="right_part",
    )(total, left)


def inverse_factor(gram):
    n = R // 8
    lane = lax.broadcasted_iota(jnp.int32, (8, R), 1)
    sub = lax.broadcasted_iota(jnp.int32, (8, R), 0)
    wide = [
        jnp.concatenate([gram[8 * i : 8 * i + 8], (lane == sub + 8 * i).astype(jnp.float32)], 1)
        for i in range(n)
    ]
    row = lax.broadcasted_iota(jnp.int32, (8, LANES), 0)
    out = []

    def pick(x, k):
        return jnp.broadcast_to(x[k : k + 1], (8, LANES))

    for p in range(n):
        column = [
            [jnp.broadcast_to(wide[i][:, 8 * p + k : 8 * p + k + 1], (8, LANES)) for i in range(p, n)]
            for k in range(8)
        ]
        scale = jnp.zeros((8, LANES), jnp.float32)
        for k in range(8):
            pivot = pick(column[k][0], k)
            times = 1.0 / pivot
            scale = jnp.where(row == k, lax.rsqrt(pivot), scale)
            by = [c * times for c in column[k]]
            by[0] = jnp.where(row > k, by[0], 0.0)
            for l in range(k + 1, 8):
                value = pick(column[l][0], k)
                column[l] = [c - b * value for c, b in zip(column[l], by)]
            value = pick(wide[p], k)
            for i in range(p, n):
                wide[i] = wide[i] - by[i - p] * value
        out.append(wide[p][:, R:] * scale[:, R:])
    return jnp.concatenate(out, 0)


def settle_kernel(parts_ref, block_ref, gram_ref):
    got = parts_ref[0]
    for b in range(1, BLOCKS):
        got = got + parts_ref[b]
    block_ref[...] = got[:R]
    gram_ref[...] = got[R:]


def settle(parts):
    return pl.pallas_call(
        settle_kernel,
        in_specs=[VMEM],
        out_specs=[VMEM, VMEM],
        out_shape=[
            jax.ShapeDtypeStruct((R, LANES), jnp.float32),
            jax.ShapeDtypeStruct((R // 2, LANES), jnp.float32),
        ],
        compiler_params=grant(6),
        name="settle",
    )(parts)


def factor_kernel(gram_ref, inverse_ref, copies_ref):
    packed = gram_ref[...]
    inverse = inverse_factor(jnp.concatenate([packed[:, :R], packed[:, R:]], 0))
    inverse_ref[...] = inverse
    for b in range(copies_ref.shape[0] // R):
        copies_ref[b * R : (b + 1) * R] = inverse


def factor(gram):
    return pl.pallas_call(
        factor_kernel,
        in_specs=[VMEM],
        out_specs=[VMEM, VMEM],
        out_shape=[
            jax.ShapeDtypeStruct((R, R), jnp.float32),
            jax.ShapeDtypeStruct((COLS // 2 * R, R), jnp.float32),
        ],
        compiler_params=grant(6),
        cost_estimate=pl.CostEstimate(flops=1, bytes_accessed=1, transcendentals=0),
        name="factor",
    )(gram)


def basis_kernel(row_ref, inverse_ref, pair0_ref, pair1_ref, pair2_ref, pair3_ref, basis_ref, round_ref):
    y = row_ref[0] // 2
    blocks = []
    for b in range(basis_ref.shape[1] // LANES):
        lanes = slice(b % 2 * LANES, (b % 2 + 1) * LANES)
        value = pair0_ref[:, lanes]
        for k, ref in enumerate((pair1_ref, pair2_ref, pair3_ref), 1):
            value = jnp.where((y + 4 - k) % 4 == b // 2, ref[:, lanes], value)
        blocks.append(value)
    basis = dot(inverse_ref[...], jnp.concatenate(blocks, 1), 1, 0, HIGHEST)
    basis_ref[...] = basis
    round_ref[...] = basis.astype(jnp.bfloat16)


def basis_part(row, inverse, pairs, units):
    return pl.pallas_call(
        basis_kernel,
        in_specs=[SMEM] + [VMEM] * 5,
        out_specs=[VMEM, VMEM],
        out_shape=[
            jax.ShapeDtypeStruct((R, units), jnp.float32),
            jax.ShapeDtypeStruct((R, units), jnp.bfloat16),
        ],
        compiler_params=grant(6),
        name="basis_part",
    )(row, inverse, *pairs)


def rollout_kernel(core_ref, left_ref, near_ref, other_ref, weight_ref, out_ref, buf, sem):
    even = core_ref[0] == 0
    width = buf.shape[2]
    copies = []
    for q in range(4):
        first, second = (near_ref, other_ref) if q % 2 == 0 else (other_ref, near_ref)
        blocks = [jnp.where(even, first[b, q // 2], second[b, q // 2]) for b in range(width // LANES)]
        delta = dot(left_ref[...], jnp.concatenate(blocks, 1), 0, 0)
        buf[q] = (weight_ref[q].astype(jnp.float32) + delta).astype(jnp.bfloat16)
        copy = pltpu.make_async_copy(buf.at[q], out_ref.at[:, pl.ds(q * width, width)], sem.at[q])
        copy.start()
        copies.append(copy)
    for copy in copies:
        copy.wait()


def rollout(core, left, near, other, weight):
    quarters, rows, width = weight.shape
    return pl.pallas_call(
        rollout_kernel,
        in_specs=[SMEM, VMEM, VMEM, VMEM, VMEM],
        out_specs=ANY,
        out_shape=jax.ShapeDtypeStruct((rows, quarters * width), jnp.bfloat16),
        scratch_shapes=[
            pltpu.VMEM((quarters, rows, width), jnp.bfloat16),
            pltpu.SemaphoreType.DMA((4,)),
        ],
        compiler_params=grant(12),
        name="rollout",
    )(core, left, near, other, weight)


def local(weight_change, error_buffer, basis, rollout_weight):
    row = lax.axis_index("row")
    q = lax.axis_index("col") % 4
    rows, units = weight_change.shape
    part = left_part(weight_change, error_buffer, basis.T)
    part, change, error = lax.optimization_barrier((part, weight_change, error_buffer))
    total = (change.astype(jnp.float32) + error).astype(jnp.bfloat16)
    parts = exchange(part.reshape(COLS, 8, rows // 4), "col")
    parts, total = lax.optimization_barrier((parts, total))
    left = exchange(sum_share(parts), "col").reshape(8, 4, 8, rows // 4)
    block, gram = settle(exchange(right_part(total, left), "row"))
    far = lax.ppermute(block, AXES, SPREAD)
    other_block = lax.ppermute(block, "row", [(r, r ^ 1) for r in range(ROWS)])
    inverse, copies = factor(gram)
    odd = row % 2 == 1
    pair = jnp.concatenate([jnp.where(odd, other_block, block), jnp.where(odd, block, other_block)], 1)
    pairs = [lax.ppermute(pair, "row", [(r, (r + 2 * k) % ROWS) for r in range(ROWS)]) for k in (1, 2, 3)]
    far_round = dot(copies, far, 1, 0, HIGH).astype(jnp.bfloat16).reshape(COLS // 2, R, LANES)
    far_round, inverse, weight, left = lax.optimization_barrier((far_round, inverse, rollout_weight, left))
    mine = lax.dynamic_index_in_dim(left, q, 1, keepdims=False).reshape(R, rows // 4)
    far_left = lax.ppermute(dot(inverse, mine, 1, 0, HIGH).astype(jnp.bfloat16), AXES, FANOUT)
    near = exchange(far_round, AXES, SAME_CORE)
    weight = jnp.stack([weight[:, i * units : (i + 1) * units] for i in range(4)])
    left_rows = left.transpose(0, 2, 1, 3).reshape(R, rows)
    left_round = dot(inverse, left_rows, 1, 0, HIGH).astype(jnp.bfloat16)
    new_basis, right_round = basis_part(row.astype(jnp.int32).reshape(1), inverse, [pair] + pairs, units)
    new_error = weight_change.astype(jnp.float32) + error_buffer - dot(left_round, right_round, 0, 0)
    near, new_error, weight, far_left = lax.optimization_barrier((near, new_error, weight, far_left))
    other = lax.ppermute(near, "col", PAIR)
    halves = (BLOCKS, 2, R, LANES)
    core = (q % 2).astype(jnp.int32).reshape(1)
    new_rollout = rollout(core, far_left, near.reshape(halves), other.reshape(halves), weight)
    return (new_error, new_basis.T, new_rollout)


def solution(mesh):
    in_specs = (P("row", "col"), P("row", "col"), P("col", None), P("col", "row"))
    out_specs = (P("row", "col"), P("col", None), P("col", "row"))
    return jax.shard_map(local, mesh=mesh, in_specs=in_specs, out_specs=out_specs, check_vma=False)
```

```python
import jax
import jax.numpy as jnp
from jax import lax
from jax.experimental import pallas as pl
from jax.experimental.pallas import tpu as pltpu
from jax.sharding import PartitionSpec as P

HIGH = lax.Precision.HIGH
HIGHEST = lax.Precision.HIGHEST
ROWS, COLS, R, LANES, BLOCKS = 8, 32, 64, 128, 8
GRAM_END = R + R // 2
AXES = ("row", "col")


def row_hops(a, b):
    y = abs(a // 2 - b // 2)
    return min(y, 4 - y) + abs(a % 2 - b % 2)


def partners(row):
    rows = sorted(range(ROWS), key=lambda r: (row_hops(r, row), r))
    places = sorted(range(8), key=lambda k: (-min(k, 8 - k), k))
    return {r: (row + k) % 8 for r, k in zip(rows, places)}


SLOTS = [[partners(z)[r] for r in range(ROWS)] for z in range(8)]
SPREAD = [
    (r * COLS + 4 * z + q, z * COLS + 4 * SLOTS[z][r] + q)
    for r in range(ROWS)
    for z in range(8)
    for q in range(4)
]
FANOUT = [
    (r * COLS + 4 * z + q, t * COLS + 4 * r + q)
    for r in range(ROWS)
    for t, z in partners(r).items()
    for q in range(4)
]
SAME_CORE = [
    [row * COLS + 4 * SLOTS[row][b] + 2 * half + core for b in range(ROWS) for half in range(2)]
    for row in range(ROWS)
    for core in range(2)
]
PAIR = [(c, c ^ 1) for c in range(COLS)]


def dot(a, b, ca, cb, precision=None):
    return lax.dot_general(
        a, b, (((ca,), (cb,)), ((), ())), precision=precision, preferred_element_type=jnp.float32
    )


def split(x):
    hi = x.astype(jnp.bfloat16)
    return hi, (x - hi.astype(jnp.float32)).astype(jnp.bfloat16)


def exchange(parts, axis, groups=None):
    return lax.all_to_all(parts, axis, 0, 0, axis_index_groups=groups)


ANY = pl.BlockSpec(memory_space=pl.ANY)
VMEM = pl.BlockSpec(memory_space=pltpu.VMEM)
SMEM = pl.BlockSpec(memory_space=pltpu.SMEM)


def grant(mib):
    return pltpu.CompilerParams(vmem_limit_bytes=mib * 2**20)


def left_kernel(change_ref, error_ref, basis_ref, out_ref, change_buf, error_buf, basis_buf, sem, basis_sem):
    rows, width = change_ref.shape[0], out_ref.shape[3]
    block = rows // 2
    basis_copy = pltpu.make_async_copy(basis_ref, basis_buf, basis_sem)
    basis_copy.start()
    copies = []
    for i in range(2):
        part = pl.ds(i * block, block)
        pair = [
            pltpu.make_async_copy(change_ref.at[part], change_buf.at[part], sem.at[0, i]),
            pltpu.make_async_copy(error_ref.at[part], error_buf.at[part], sem.at[1, i]),
        ]
        for copy in pair:
            copy.start()
        copies.append(pair)
    basis_copy.wait()
    basis_hi, basis_lo = split(basis_buf[...])
    basis_both = jnp.concatenate([basis_hi, basis_lo], 0)
    for i in range(2):
        for copy in copies[i]:
            copy.wait()
        part = pl.ds(i * block, block)
        hi, lo = split(change_buf[part].astype(jnp.float32) + error_buf[part])
        both = dot(basis_both, hi, 1, 1)
        left = both[:R] + both[R:] + dot(basis_hi, lo, 1, 1)
        for j in range(block // width):
            out_ref[:, i * (block // width) + j] = left[:, j * width : (j + 1) * width].reshape(8, 8, width)


def left_part(change, error, basis):
    rows, units = change.shape
    return pl.pallas_call(
        left_kernel,
        in_specs=[ANY, ANY, ANY],
        out_specs=VMEM,
        out_shape=jax.ShapeDtypeStruct((8, 4, 8, rows // 4), jnp.float32),
        scratch_shapes=[
            pltpu.VMEM((rows, units), jnp.bfloat16),
            pltpu.VMEM((rows, units), jnp.float32),
            pltpu.VMEM((R, units), jnp.float32),
            pltpu.SemaphoreType.DMA((2, 2)),
            pltpu.SemaphoreType.DMA,
        ],
        compiler_params=grant(62),
        cost_estimate=pl.CostEstimate(flops=6 * rows * units * R, bytes_accessed=6 * rows * units, transcendentals=0),
        name="left_part",
    )(change, error, basis)


def sum_share_kernel(parts_ref, out_ref):
    total = parts_ref[0]
    for i in range(1, parts_ref.shape[0]):
        total = total + parts_ref[i]
    for i in range(out_ref.shape[0]):
        out_ref[i] = total


def sum_share(parts):
    return pl.pallas_call(
        sum_share_kernel,
        in_specs=[VMEM],
        out_specs=VMEM,
        out_shape=jax.ShapeDtypeStruct(parts.shape, parts.dtype),
        compiler_params=grant(6),
        name="sum_share",
    )(parts)


def right_kernel(total_ref, left_ref, out_ref):
    left = jnp.concatenate([left_ref[:, i].reshape(R, -1) for i in range(4)], 1)
    both = dot(jnp.concatenate(split(left), 0), total_ref[...], 1, 0)
    right = both[:R] + both[R:]
    used = right.shape[1] // LANES
    for b in range(used):
        out_ref[b, :R] = right[:, b * LANES : (b + 1) * LANES]
    for b in range(used, BLOCKS):
        out_ref[b, :R] = jnp.zeros((R, LANES), jnp.float32)
    gram = dot(left, left, 1, 1, HIGHEST)
    for b in range(BLOCKS):
        out_ref[b, R : GRAM_END, :R] = gram[: R // 2]
        out_ref[b, R : GRAM_END, R:] = gram[R // 2 :]


def right_part(total, left):
    rows, units = total.shape
    return pl.pallas_call(
        right_kernel,
        in_specs=[VMEM, VMEM],
        out_specs=VMEM,
        out_shape=jax.ShapeDtypeStruct((BLOCKS, GRAM_END, LANES), jnp.float32),
        compiler_params=grant(12),
        cost_estimate=pl.CostEstimate(flops=4 * rows * units * R, bytes_accessed=2 * rows * units, transcendentals=0),
        name="right_part",
    )(total, left)


def inverse_factor(gram):
    n = R // 8
    lane = lax.broadcasted_iota(jnp.int32, (8, R), 1)
    sub = lax.broadcasted_iota(jnp.int32, (8, R), 0)
    wide = [
        jnp.concatenate([gram[8 * i : 8 * i + 8], (lane == sub + 8 * i).astype(jnp.float32)], 1)
        for i in range(n)
    ]
    row = lax.broadcasted_iota(jnp.int32, (8, LANES), 0)
    out = []

    def pick(x, k):
        return jnp.broadcast_to(x[k : k + 1], (8, LANES))

    for p in range(n):
        column = [
            [jnp.broadcast_to(wide[i][:, 8 * p + k : 8 * p + k + 1], (8, LANES)) for i in range(p, n)]
            for k in range(8)
        ]
        scale = jnp.zeros((8, LANES), jnp.float32)
        for k in range(8):
            pivot = pick(column[k][0], k)
            times = 1.0 / pivot
            scale = jnp.where(row == k, lax.rsqrt(pivot), scale)
            by = [c * times for c in column[k]]
            by[0] = jnp.where(row > k, by[0], 0.0)
            for l in range(k + 1, 8):
                value = pick(column[l][0], k)
                column[l] = [c - b * value for c, b in zip(column[l], by)]
            value = pick(wide[p], k)
            for i in range(p, n):
                wide[i] = wide[i] - by[i - p] * value
        out.append(wide[p][:, R:] * scale[:, R:])
    return jnp.concatenate(out, 0)


def settle_kernel(parts_ref, block_ref, gram_ref):
    got = parts_ref[0]
    for b in range(1, BLOCKS):
        got = got + parts_ref[b]
    block_ref[...] = got[:R]
    gram_ref[...] = got[R:]


def settle(parts):
    return pl.pallas_call(
        settle_kernel,
        in_specs=[VMEM],
        out_specs=[VMEM, VMEM],
        out_shape=[
            jax.ShapeDtypeStruct((R, LANES), jnp.float32),
            jax.ShapeDtypeStruct((R // 2, LANES), jnp.float32),
        ],
        compiler_params=grant(6),
        name="settle",
    )(parts)


def factor_kernel(gram_ref, inverse_ref, copies_ref):
    packed = gram_ref[...]
    inverse = inverse_factor(jnp.concatenate([packed[:, :R], packed[:, R:]], 0))
    inverse_ref[...] = inverse
    for b in range(copies_ref.shape[0] // R):
        copies_ref[b * R : (b + 1) * R] = inverse


def factor(gram):
    return pl.pallas_call(
        factor_kernel,
        in_specs=[VMEM],
        out_specs=[VMEM, VMEM],
        out_shape=[
            jax.ShapeDtypeStruct((R, R), jnp.float32),
            jax.ShapeDtypeStruct((COLS // 2 * R, R), jnp.float32),
        ],
        compiler_params=grant(6),
        cost_estimate=pl.CostEstimate(flops=1, bytes_accessed=1, transcendentals=0),
        name="factor",
    )(gram)


def basis_kernel(row_ref, inverse_ref, pair0_ref, pair1_ref, pair2_ref, pair3_ref, basis_ref, round_ref):
    y = row_ref[0] // 2
    blocks = []
    for b in range(basis_ref.shape[1] // LANES):
        lanes = slice(b % 2 * LANES, (b % 2 + 1) * LANES)
        value = pair0_ref[:, lanes]
        for k, ref in enumerate((pair1_ref, pair2_ref, pair3_ref), 1):
            value = jnp.where((y + 4 - k) % 4 == b // 2, ref[:, lanes], value)
        blocks.append(value)
    basis = dot(inverse_ref[...], jnp.concatenate(blocks, 1), 1, 0, HIGHEST)
    basis_ref[...] = basis
    round_ref[...] = basis.astype(jnp.bfloat16)


def basis_part(row, inverse, pairs, units):
    return pl.pallas_call(
        basis_kernel,
        in_specs=[SMEM] + [VMEM] * 5,
        out_specs=[VMEM, VMEM],
        out_shape=[
            jax.ShapeDtypeStruct((R, units), jnp.float32),
            jax.ShapeDtypeStruct((R, units), jnp.bfloat16),
        ],
        compiler_params=grant(6),
        name="basis_part",
    )(row, inverse, *pairs)


def rollout_kernel(core_ref, left_ref, near_ref, other_ref, weight_ref, out_ref, buf, sem):
    even = core_ref[0] == 0
    width = buf.shape[2]
    copies = []
    for q in range(4):
        first, second = (near_ref, other_ref) if q % 2 == 0 else (other_ref, near_ref)
        blocks = [jnp.where(even, first[b, q // 2], second[b, q // 2]) for b in range(width // LANES)]
        delta = dot(left_ref[...], jnp.concatenate(blocks, 1), 0, 0)
        buf[q] = (weight_ref[q].astype(jnp.float32) + delta).astype(jnp.bfloat16)
        copy = pltpu.make_async_copy(buf.at[q], out_ref.at[:, pl.ds(q * width, width)], sem.at[q])
        copy.start()
        copies.append(copy)
    for copy in copies:
        copy.wait()


def rollout(core, left, near, other, weight):
    quarters, rows, width = weight.shape
    return pl.pallas_call(
        rollout_kernel,
        in_specs=[SMEM, VMEM, VMEM, VMEM, VMEM],
        out_specs=ANY,
        out_shape=jax.ShapeDtypeStruct((rows, quarters * width), jnp.bfloat16),
        scratch_shapes=[
            pltpu.VMEM((quarters, rows, width), jnp.bfloat16),
            pltpu.SemaphoreType.DMA((4,)),
        ],
        compiler_params=grant(12),
        name="rollout",
    )(core, left, near, other, weight)


def local(weight_change, error_buffer, basis, rollout_weight):
    row = lax.axis_index("row")
    q = lax.axis_index("col") % 4
    rows, units = weight_change.shape
    part = left_part(weight_change, error_buffer, basis.T)
    part, change, error = lax.optimization_barrier((part, weight_change, error_buffer))
    total = (change.astype(jnp.float32) + error).astype(jnp.bfloat16)
    parts = exchange(part.reshape(COLS, 8, rows // 4), "col")
    parts, total = lax.optimization_barrier((parts, total))
    left = exchange(sum_share(parts), "col").reshape(8, 4, 8, rows // 4)
    block, gram = settle(exchange(right_part(total, left), "row"))
    far = lax.ppermute(block, AXES, SPREAD)
    other_block = lax.ppermute(block, "row", [(r, r ^ 1) for r in range(ROWS)])
    inverse, copies = factor(gram)
    odd = row % 2 == 1
    pair = jnp.concatenate([jnp.where(odd, other_block, block), jnp.where(odd, block, other_block)], 1)
    pairs = [lax.ppermute(pair, "row", [(r, (r + 2 * k) % ROWS) for r in range(ROWS)]) for k in (1, 2, 3)]
    far_round = dot(copies, far, 1, 0, HIGH).astype(jnp.bfloat16).reshape(COLS // 2, R, LANES)
    far_round, inverse, weight, left = lax.optimization_barrier((far_round, inverse, rollout_weight, left))
    mine = lax.dynamic_index_in_dim(left, q, 1, keepdims=False).reshape(R, rows // 4)
    near = exchange(far_round, AXES, SAME_CORE)
    weight = jnp.stack([weight[:, i * units : (i + 1) * units] for i in range(4)])
    weight, mine = lax.optimization_barrier((weight, mine))
    far_left = lax.ppermute(dot(inverse, mine, 1, 0, HIGH).astype(jnp.bfloat16), AXES, FANOUT)
    left_rows = left.transpose(0, 2, 1, 3).reshape(R, rows)
    left_round = dot(inverse, left_rows, 1, 0, HIGH).astype(jnp.bfloat16)
    new_basis, right_round = basis_part(row.astype(jnp.int32).reshape(1), inverse, [pair] + pairs, units)
    new_error = weight_change.astype(jnp.float32) + error_buffer - dot(left_round, right_round, 0, 0)
    near, new_error, weight, far_left = lax.optimization_barrier((near, new_error, weight, far_left))
    other = lax.ppermute(near, "col", PAIR)
    halves = (BLOCKS, 2, R, LANES)
    core = (q % 2).astype(jnp.int32).reshape(1)
    new_rollout = rollout(core, far_left, near.reshape(halves), other.reshape(halves), weight)
    return (new_error, new_basis.T, new_rollout)


def solution(mesh):
    in_specs = (P("row", "col"), P("row", "col"), P("col", None), P("col", "row"))
    out_specs = (P("row", "col"), P("col", None), P("col", "row"))
    return jax.shard_map(local, mesh=mesh, in_specs=in_specs, out_specs=out_specs, check_vma=False)
```
